32 devices in a mesh: run: 2 (over y), tile: 4 (over z), sub: 2 (over x), pair: 2 (over core).
Axes of the slice: x: 2, y: 2, z: 4, core: 2. Of those that a mesh axis runs over, the one named last changes fastest.
Arguments:
- induction_vector: float32 [3, 4, 32, 512], P(None, ('run', 'pair'), ('tile', 'sub')), parts along dimension 1, may hold values from -6 to 6
- ohmic_spreading_number: float32 [4, 32, 512], P(('run', 'pair'), ('tile', 'sub')), parts along dimension 0, may hold values from 0.03 to 0.15
- reciprocal_surface: float32 [4, 32, 512], P(('run', 'pair'), ('tile', 'sub')), parts along dimension 0, may hold values from 0.5 to 2
- number_per_volume: float32 [4, 32, 512], P(('run', 'pair'), ('tile', 'sub')), parts along dimension 0, may hold values from 0.2 to 2
- thermal_kelvin: float32 [4, 32, 512], P(('run', 'pair'), ('tile', 'sub')), parts along dimension 0, may hold values from 0.5 to 4
- mapped_brick_members: int32 [4, 8, 8, 512], P(('run', 'pair'), ('tile', 'sub')), parts along dimension 0, may hold values from -1 to 2047, as said below
- arrival_owner_map: int32 [4, 8, 8, 512], P(('run', 'pair'), ('tile', 'sub')), parts along dimension 0, may hold values from 0 to 1023
- pedersen_sheet: float32 [64, 16, 512], P(('run', 'pair'), ('tile', 'sub')), parts along dimension 0, as said below
- electric_decay_rate: float32 [32, 512], P(('run', 'tile', 'sub')), parts along dimension 0, may hold values from 0.2 to 4
Outputs:
- advanced_field: float32 [3, 4, 32, 512], P(None, ('run', 'pair'), ('tile', 'sub')), parts along dimension 1
- boundary: float32 [2, 4, 32, 512], P(None, ('run', 'pair'), ('tile', 'sub')), parts along dimension 1
- potential: float32 [32, 512], P(('run', 'tile', 'sub')), parts along dimension 0
The draws below stay inside these ranges and needn't reach their ends.
There are 2 independent parts, one for each index of `run`. The reference program is written for one: setup_inputs(seed, part) draws one part's arguments, and reference() takes and returns one part's arrays. A program takes and returns all parts, laid end to end along the dimension named above; each array names one. Nothing has to cross between parts.
Inputs may be any that keep to these rules, and one draw needn't show every extreme that they name: mapped_brick_members[p, s, d] lists cells of brick (p, s) whose field lines land on device d, -1 in empty slots; no cell appears twice among one brick's lists; in each run one device d receives exactly 512 cells from every brick. `pedersen_sheet`: positive.
All inputs are finite; a program needn't handle non-finite values.
Results may differ from the reference program's by a relative error of at most 0.00002.
Values sent between devices are 32-bit elements; how exact they have to be, the bound alone decides.
No kernel may reach another device: no remote copies, remote signals or barrier semaphores. Data moves between devices by JAX's collectives and lax.ppermute only.
A program may use at most 64 MiB of HBM per device.

```python
import math
import jax
import jax.numpy as jnp
from jax import lax

SH_DEV = 1
TH_DEV = 4
EASTWARD_BINS = 512
LON = 512
DIFF_STEPS = 4
SWEEPS = 8
PAIRS = 2
TILES = 4
SUBS = 2
NION = 8
SPAN_LAYERS = 2
COLATITUDE_BINS = 32
LAT = 16
LEVELS = 32
CELLS = 2048
COLS = 1024
CAP = 512


def draw_mapped_brick_members(key, part):
    key = jax.random.fold_in(key, 5)
    key_hot, key_side, key_order, key_dest = jax.random.split(key, 4)
    tile_index = jnp.arange(TILES, dtype=jnp.int32)
    distance = jnp.abs(2 * tile_index + 1 - TILES)
    tile_weight = 1 + 7 * distance ** 4 // TILES ** 4
    dest_weight = jnp.repeat(tile_weight, SUBS)
    bounds = jnp.cumsum(dest_weight)
    senders = PAIRS * NION
    hot_tile = jnp.where(jax.random.randint(key_side, (), 0, 2) == 1, TILES - 1, 0)
    hot_peer = hot_tile * SUBS + jax.random.randint(key_hot, (), 0, SUBS)
    order_keys = jax.random.split(key_order, senders)
    cell_order = jax.vmap(lambda order_key: jax.random.permutation(order_key, CELLS))(order_keys)
    position = jnp.argsort(cell_order, axis=1).astype(jnp.int32)
    dest_draws = jax.random.randint(key_dest, (senders, CELLS), 0, bounds[-1])
    random_dest = jnp.searchsorted(bounds, dest_draws, side='right').astype(jnp.int32)
    destination = jnp.where(position < CAP, hot_peer, random_dest).astype(jnp.int32)
    sort_key = destination * CELLS + position
    ranked = jnp.argsort(sort_key, axis=1).astype(jnp.int32)
    sorted_dest = jnp.take_along_axis(destination, ranked, axis=1)
    counts = jax.vmap(lambda dest_row: jnp.zeros((NION,), jnp.int32).at[dest_row].add(1))(destination)
    starts = jnp.cumsum(counts, axis=1) - counts
    slot_index = jnp.arange(CELLS, dtype=jnp.int32)[None, :] - jnp.take_along_axis(starts, sorted_dest, axis=1)
    slot_index = jnp.where(slot_index < CAP, slot_index, CAP)
    sender_index = jnp.broadcast_to(jnp.arange(senders, dtype=jnp.int32)[:, None], (senders, CELLS))
    cell_lists = jnp.full((senders, NION, CAP), -1, jnp.int32).at[sender_index, sorted_dest, slot_index].set(ranked, mode='drop')
    return cell_lists.reshape(PAIRS, NION, NION, CAP)


def draw_pedersen_sheet(key, part):
    key = jax.random.fold_in(key, 11)
    key_level = jax.random.fold_in(key, 0)
    level = jnp.arange(LEVELS).astype(jnp.float32)
    profile = 3.0 / LEVELS * jnp.exp(-2.5 * (level + 0.5) / LEVELS)
    factor = jnp.exp(jax.random.uniform(key_level, (LEVELS, LAT, LON), jnp.float32, jnp.log(0.3), jnp.log(3.0)))
    return profile[:, None, None] * factor


def plant(drawn, stream_key, smallest, top_value):
    longest = drawn.shape.index(max(drawn.shape))
    spots = []
    for shift in (0, 1):
        where = [jax.random.randint(jax.random.fold_in(stream_key, axis), (), 0, length) for axis, length in enumerate(drawn.shape)]
        where[longest] = (where[longest] + shift) % drawn.shape[longest]
        spots.append(tuple(where))
    return drawn.at[spots[0]].set(smallest).at[spots[1]].set(top_value)


def level_of(key, dims, pieces, low, high):
    gain = 1.0
    for dim, shards_of in pieces:
        steps = jax.random.uniform(jax.random.fold_in(jax.random.fold_in(key, 6), dim), (shards_of,), jnp.float32, low / len(pieces), high / len(pieces))
        gain = gain * jnp.repeat(jnp.exp(steps), dims[dim] // shards_of).reshape((-1,) + (1,) * (len(dims) - 1 - dim))
    return gain


def noise(own_key, extent, deviation, limit, cuts=(), held_as=jnp.bfloat16):
    entries = jax.random.normal(own_key, extent, jnp.float32) * deviation
    if len(cuts) > 0:
        entries = level_of(own_key, extent, cuts, -0.22, 0.18) * entries
    return jnp.clip(entries, min=-limit, max=limit).astype(held_as)


def setup_inputs(seed: int = 0, part: int = 0) -> dict:
    seeds = jax.random.split(jax.random.key(seed), 10)
    own_keys = jax.random.split(jax.random.fold_in(seeds[9], part), 10)
    return {
        "induction_vector": noise(own_keys[0], (3, SPAN_LAYERS, COLATITUDE_BINS, EASTWARD_BINS), 1.0, 6.0, ((1, 2), (2, 8)), jnp.float32),
        "ohmic_spreading_number": jnp.clip(jnp.exp(math.log(0.15) - 1.609438 * jax.random.uniform(own_keys[1], (SPAN_LAYERS, COLATITUDE_BINS, EASTWARD_BINS), jnp.float32) ** level_of(own_keys[1], (SPAN_LAYERS, COLATITUDE_BINS, EASTWARD_BINS), ((0, 2), (1, 8)), -0.2, 0.2)), 0.03, 0.15),
        "reciprocal_surface": jnp.clip(jnp.exp(math.log(2.0) - 1.3862944 * jax.random.uniform(own_keys[2], (SPAN_LAYERS, COLATITUDE_BINS, EASTWARD_BINS), jnp.float32) ** level_of(own_keys[2], (SPAN_LAYERS, COLATITUDE_BINS, EASTWARD_BINS), ((0, 2), (1, 8)), -0.2, 0.2)), 0.5, 2.0),
        "number_per_volume": jnp.clip(jnp.exp(math.log(2.0) - 2.3025851 * jax.random.uniform(own_keys[3], (SPAN_LAYERS, COLATITUDE_BINS, EASTWARD_BINS), jnp.float32) ** level_of(own_keys[3], (SPAN_LAYERS, COLATITUDE_BINS, EASTWARD_BINS), ((0, 2), (1, 8)), -0.2, 0.2)), 0.2, 2.0),
        "thermal_kelvin": jnp.clip(jnp.exp(math.log(4.0) - 2.0794415 * jax.random.uniform(own_keys[4], (SPAN_LAYERS, COLATITUDE_BINS, EASTWARD_BINS), jnp.float32) ** level_of(own_keys[4], (SPAN_LAYERS, COLATITUDE_BINS, EASTWARD_BINS), ((0, 2), (1, 8)), -0.2, 0.2)), 0.5, 4.0),
        "mapped_brick_members": draw_mapped_brick_members(jax.random.fold_in(jax.random.fold_in(seeds[9], part), 71), part),
        "arrival_owner_map": plant(jax.random.randint(own_keys[6], (PAIRS, NION, NION, CAP), 0, COLS), jax.random.fold_in(own_keys[6], 1), 0, COLS - 1).astype(jnp.int32),
        "pedersen_sheet": draw_pedersen_sheet(jax.random.fold_in(jax.random.fold_in(seeds[9], part), 71), part),
        "electric_decay_rate": jnp.clip(jnp.exp(math.log(4.0) - 2.9957323 * jax.random.uniform(own_keys[8], (LAT, LON), jnp.float32) ** level_of(own_keys[8], (LAT, LON), ((0, 8),), -0.2, 0.2)), 0.2, 4.0),
    }


def advance_field(current_state, ohmic_spreading_number):
    padded = jnp.pad(current_state, ((0, 0), (1, 1), (1, 1), (0, 0)))
    neighbours = padded[:, 2:, 1:-1] + padded[:, :-2, 1:-1] + padded[:, 1:-1, 2:] + padded[:, 1:-1, :-2]
    neighbours = neighbours + jnp.roll(current_state, -1, 3) + jnp.roll(current_state, 1, 3)
    return current_state + ohmic_spreading_number * (neighbours - 6.0 * current_state)

def to_blocks(values):
    values = values.reshape(PAIRS, SH_DEV, NION, TH_DEV, EASTWARD_BINS)
    return jnp.transpose(values, (0, 2, 1, 3, 4)).reshape(PAIRS, NION, CELLS)

def from_blocks(values):
    values = values.reshape(PAIRS, NION, SH_DEV, TH_DEV, EASTWARD_BINS)
    return jnp.transpose(values, (0, 2, 1, 3, 4)).reshape(SPAN_LAYERS, COLATITUDE_BINS, EASTWARD_BINS)

def reference(induction_vector, ohmic_spreading_number, reciprocal_surface, number_per_volume, thermal_kelvin, mapped_brick_members, arrival_owner_map, pedersen_sheet, electric_decay_rate):
    phi_padded = jnp.pad(induction_vector[2], ((0, 0), (1, 1), (0, 0)))
    theta_diff = phi_padded[:, 2:] - phi_padded[:, :-2]
    phi_diff = jnp.roll(induction_vector[1], -1, 2) - jnp.roll(induction_vector[1], 1, 2)
    current = 0.5 * reciprocal_surface * (theta_diff - phi_diff)
    precipitation_power = 0.25 * number_per_volume * jnp.sqrt(thermal_kelvin)
    sources = jnp.stack([to_blocks(current), to_blocks(precipitation_power)])
    is_listed = mapped_brick_members >= 0
    safe_index = jnp.where(is_listed, mapped_brick_members, 0).astype(jnp.int32).reshape(PAIRS, NION, NION * CAP)
    picked = jax.vmap(lambda source_block: jnp.take_along_axis(source_block, safe_index, axis=2))(sources)
    sent_terms = jnp.where(is_listed[None], picked.reshape(2, PAIRS, NION, NION, CAP), 0.0)
    arrived = jnp.transpose(sent_terms, (0, 1, 3, 2, 4))
    pair_index = jnp.arange(PAIRS, dtype=jnp.int32)[:, None, None, None]
    device_index = jnp.arange(NION, dtype=jnp.int32)[None, :, None, None]
    target = ((pair_index * NION + device_index) * COLS + arrival_owner_map).astype(jnp.int32)
    column_terms = jax.vmap(lambda values: jax.ops.segment_sum(values.reshape(-1), target.reshape(-1), num_segments=PAIRS * NION * COLS))(arrived)
    column_terms = lax.optimization_barrier(jnp.sum(column_terms.reshape(2, PAIRS, LAT, LON), axis=1))
    aligned_current = column_terms[0]
    conductance = lax.optimization_barrier(jnp.sum(pedersen_sheet, axis=0)) + column_terms[1]
    cond_rim = jnp.pad(conductance, ((1, 1), (0, 0)))
    north_face = 0.5 * (conductance + cond_rim[:-2])
    south_face = 0.5 * (conductance + cond_rim[2:])
    east_face = 0.5 * (conductance + jnp.roll(conductance, -1, 1))
    west_face = 0.5 * (conductance + jnp.roll(conductance, 1, 1))
    diagonal = electric_decay_rate + north_face + south_face + east_face + west_face
    potential = aligned_current / diagonal
    for sweep_index in range(SWEEPS - 1):
        potential_rim = jnp.pad(potential, ((1, 1), (0, 0)))
        potential = (aligned_current + north_face * potential_rim[:-2] + south_face * potential_rim[2:] + east_face * jnp.roll(potential, -1, 1) + west_face * jnp.roll(potential, 1, 1)) / diagonal
    column_values = jnp.stack([potential, conductance]).reshape(2, NION, COLS)
    land_index = jnp.transpose(arrival_owner_map, (1, 0, 2, 3)).reshape(NION, PAIRS * NION * CAP).astype(jnp.int32)
    fetched = jax.vmap(lambda values: jnp.take_along_axis(values, land_index, axis=1))(column_values)
    fetched = jnp.transpose(fetched.reshape(2, NION, PAIRS, NION, CAP), (0, 2, 1, 3, 4))
    returned = jnp.transpose(fetched, (0, 1, 3, 2, 4))
    sender_base = (jnp.arange(PAIRS, dtype=jnp.int32)[:, None, None, None] * NION + jnp.arange(NION, dtype=jnp.int32)[None, :, None, None]) * CELLS
    place_index = jnp.where(is_listed, sender_base + mapped_brick_members, PAIRS * NION * CELLS).astype(jnp.int32)
    placed = jnp.zeros((2, PAIRS * NION * CELLS), jnp.float32).at[:, place_index.reshape(-1)].add(returned.reshape(2, -1), mode='drop')
    placed = placed.reshape(2, PAIRS, NION, CELLS)
    boundary = jnp.stack([from_blocks(placed[0]), from_blocks(placed[1])])
    advanced = induction_vector
    for step_index in range(DIFF_STEPS):
        advanced = advance_field(advanced, ohmic_spreading_number)
    return (advanced, boundary, potential)
```

```python
import functools

import jax
import jax.numpy as jnp
from jax import lax
from jax.experimental import pallas as pl
from jax.experimental.pallas import tpu as pltpu
from jax.sharding import PartitionSpec as P

DIFF_STEPS = 4
SWEEPS = 8


def extended(cells, sides, width):
    for axis, dim in sides:
        count = lax.axis_size(axis)
        ends = count - 1
        head = lax.slice_in_dim(cells, 0, width, axis=dim)
        tail = lax.slice_in_dim(cells, cells.shape[dim] - width, cells.shape[dim], axis=dim)
        cells = jnp.concatenate(
            [
                lax.ppermute(tail, axis, [(i, (i + 1) % count) for i in range(ends)]),
                cells,
                lax.ppermute(head, axis, [((i + 1) % count, i) for i in range(ends)]),
            ],
            axis=dim,
        )
    return cells


def extend_cells(current_state):
    return extended(current_state, ((("tile", "sub"), 2), ("pair", 1)), 1)


def extend_columns(grid_values):
    return extended(grid_values, ((("tile", "sub"), 0),), 1)


def advance_field(current_state, padded, ohmic_spreading_number):
    neighbours = (
        padded[:, 2:, 1:-1] + padded[:, :-2, 1:-1] + padded[:, 1:-1, 2:] + padded[:, 1:-1, :-2]
    )
    neighbours = neighbours + jnp.roll(current_state, -1, 3) + jnp.roll(current_state, 1, 3)
    return current_state + ohmic_spreading_number * (neighbours - 6.0 * current_state)


def stepwise(
    induction_vector,
    ohmic_spreading_number,
    reciprocal_surface,
    number_per_volume,
    thermal_kelvin,
    mapped_brick_members,
    arrival_owner_map,
    pedersen_sheet,
    electric_decay_rate,
):
    padded = extend_cells(induction_vector)
    theta_diff = padded[2, 1:-1, 2:] - padded[2, 1:-1, :-2]
    phi_diff = jnp.roll(induction_vector[1], -1, 2) - jnp.roll(induction_vector[1], 1, 2)
    current = 0.5 * reciprocal_surface * (theta_diff - phi_diff)
    precipitation_power = 0.25 * number_per_volume * jnp.sqrt(thermal_kelvin)
    cell_lists = mapped_brick_members[0, 0]
    is_listed = cell_lists >= 0
    safe_index = jnp.where(is_listed, cell_lists, 0)
    sources = jnp.stack([current.reshape(-1), precipitation_power.reshape(-1)])
    payload = jnp.where(is_listed[None], sources[:, safe_index], 0.0)
    arrived = lax.all_to_all(payload, ("tile", "sub"), split_axis=1, concat_axis=1, tiled=True)
    land_columns = arrival_owner_map[0, 0]
    lat_rows, lon_cells = electric_decay_rate.shape
    column_count = lat_rows * lon_cells
    column_terms = (
        jnp.zeros((2, column_count), jnp.float32)
        .at[:, land_columns.reshape(-1)]
        .add(arrived.reshape(2, -1))
    )
    local_conductance = jnp.sum(pedersen_sheet, axis=0) + column_terms[1].reshape(
        lat_rows, lon_cells
    )
    aligned_current, conductance = lax.psum(
        (column_terms[0].reshape(lat_rows, lon_cells), local_conductance), "pair"
    )
    advanced = advance_field(induction_vector, padded, ohmic_spreading_number)
    for step_index in range(1, DIFF_STEPS):
        advanced = advance_field(advanced, extend_cells(advanced), ohmic_spreading_number)
    cond_rim = extend_columns(conductance)
    north_face = 0.5 * (conductance + cond_rim[:-2])
    south_face = 0.5 * (conductance + cond_rim[2:])
    east_face = 0.5 * (conductance + jnp.roll(conductance, -1, 1))
    west_face = 0.5 * (conductance + jnp.roll(conductance, 1, 1))
    diagonal = electric_decay_rate + north_face + south_face + east_face + west_face
    potential = aligned_current / diagonal
    for sweep_index in range(SWEEPS - 1):
        potential_rim = extend_columns(potential)
        potential = (
            aligned_current
            + north_face * potential_rim[:-2]
            + south_face * potential_rim[2:]
            + east_face * jnp.roll(potential, -1, 1)
            + west_face * jnp.roll(potential, 1, 1)
        ) / diagonal
    column_values = jnp.stack([potential, conductance]).reshape(2, -1)
    returned = lax.all_to_all(
        column_values[:, land_columns], ("tile", "sub"), split_axis=1, concat_axis=1, tiled=True
    )
    cell_count = current.size
    target = jnp.where(is_listed, cell_lists, cell_count)
    boundary = jnp.zeros((2, cell_count), jnp.float32).at[:, target].add(returned, mode="drop")
    boundary = boundary.reshape((2,) + current.shape)
    return (advanced, boundary, potential)


LANES = 128
PEERS = 8
RING = ("tile", "sub")
GROUP = ("tile", "sub", "pair")
CURRENT, FLUX, RIM_WEIGHT, CELL, OWNER, FIRST_ROW, LAST_ROW, DECAY = range(8)
CHUNK_FIELDS = 10


def pick_lanes(row, lane):
    return jnp.take_along_axis(
        jnp.broadcast_to(row, lane.shape), lane, axis=1, mode="promise_in_bounds"
    )


def blocks_of(count):
    return [slice(b * LANES, (b + 1) * LANES) for b in range(count)]


def field_rows(field, block, blocks):
    return pl.ds(field * blocks + block, PEERS, stride=CHUNK_FIELDS * blocks)


def three_terms(values):
    first = values.astype(jnp.bfloat16)
    rest = values - first.astype(jnp.float32)
    second = rest.astype(jnp.bfloat16)
    third = (rest - second.astype(jnp.float32)).astype(jnp.bfloat16)
    return first, second, third


def one_hot_sums(rows, lanes, terms, row_count):
    total = None
    slots = rows.shape[1]
    row_at = lax.broadcasted_iota(jnp.int32, (row_count, slots), 0)
    lane_at = lax.broadcasted_iota(jnp.int32, (LANES, slots), 0)
    for s in range(rows.shape[0]):
        here = row_at == rows[s : s + 1]
        left = jnp.concatenate(
            [
                jnp.where(here, jnp.broadcast_to(t[s : s + 1], here.shape), 0.0)
                for t in terms
            ],
            axis=0,
        ).astype(jnp.bfloat16)
        right = jnp.where(lane_at == lanes[s : s + 1], 1.0, 0.0).astype(jnp.bfloat16)
        part = lax.dot_general(
            left, right, (((1,), (1,)), ((), ())), preferred_element_type=jnp.float32
        )
        total = part if total is None else total + part
    return total


def collect_kernel(field, reciprocal, number, kelvin, lists, owners, decay, sent, packet):
    theta_rows, lon = reciprocal.shape[1:]
    blocks = lon // LANES
    toward_theta = field[2, 0]
    toward_phi = field[1, 0]
    zero_row = jnp.zeros((1, lon), jnp.float32)
    half = 0.5 * reciprocal[0]
    theta_diff = jnp.concatenate([toward_theta[1:], zero_row], 0) - jnp.concatenate(
        [zero_row, toward_theta[:-1]], 0
    )
    phi_diff = pltpu.roll(toward_phi, lon - 1, 1) - pltpu.roll(toward_phi, 1, 1)
    current = half * (theta_diff - phi_diff)
    flux = 0.25 * number[0] * jnp.sqrt(kelvin[0])
    for b, span in enumerate(blocks_of(blocks)):
        cell = lists[:, span]
        lane = cell & (LANES - 1)
        row = cell >> 7
        taken = [jnp.zeros(cell.shape, jnp.float32)] * 3
        for theta in range(theta_rows):
            for c, source in enumerate(blocks_of(blocks)):
                here = row == theta * blocks + c
                at = slice(theta, theta + 1)
                tables = [current[at, source], flux[at, source]]
                if theta == 0:
                    tables.append(-half[at, source])
                if theta == theta_rows - 1:
                    tables.append(half[at, source])
                for k, table in enumerate(tables):
                    taken[k] = jnp.where(here, pick_lanes(table, lane), taken[k])
        values = taken + [cell.astype(jnp.float32), owners[:, span].astype(jnp.float32)]
        values += [
            jnp.broadcast_to(r[:, span], cell.shape)
            for r in (toward_theta[:1], toward_theta[-1:], decay[0:1], decay[1:2])
        ]
        values.append(jnp.zeros(cell.shape, jnp.float32))
        for k, value in enumerate(values):
            sent[field_rows(k, b, blocks), :] = value
    for k in range(3):
        packet[k * theta_rows : (k + 1) * theta_rows] = field[k, 0]


def deposit_kernel(arrived, owners, sheet, sums):
    lon = sheet.shape[-1]
    blocks = lon // LANES
    lat_rows = sheet.shape[1]
    peer = lax.broadcasted_iota(jnp.int32, (PEERS, LANES), 0)
    above, below = [], []
    for b in range(blocks):
        last = pltpu.roll(arrived[field_rows(LAST_ROW, b, blocks), :], 1, 0)
        above.append(jnp.where(peer == 0, 0.0, last))
        first = pltpu.roll(arrived[field_rows(FIRST_ROW, b, blocks), :], PEERS - 1, 0)
        below.append(jnp.where(peer == PEERS - 1, 0.0, first))
    currents, fluxes = [], []
    for b in range(blocks):
        cell = arrived[field_rows(CELL, b, blocks), :].astype(jnp.int32)
        phi_block = (cell >> 7) & (blocks - 1)
        lane = cell & (LANES - 1)
        rim = jnp.zeros((PEERS, LANES), jnp.float32)
        for c in range(blocks):
            found = jnp.where(
                cell < lon, pick_lanes(above[c], lane), pick_lanes(below[c], lane)
            )
            rim = jnp.where(phi_block == c, found, rim)
        weight = arrived[field_rows(RIM_WEIGHT, b, blocks), :]
        currents.append(arrived[field_rows(CURRENT, b, blocks), :] + weight * rim)
        fluxes.append(arrived[field_rows(FLUX, b, blocks), :])
    column = owners[...]
    terms = three_terms(jnp.concatenate(currents, 1)) + three_terms(jnp.concatenate(fluxes, 1))
    rows = lat_rows * blocks
    total = one_hot_sums(
        column >> 7, column & (LANES - 1), [t.astype(jnp.float32) for t in terms], rows
    )
    parts = [total[k * rows : (k + 1) * rows] for k in range(6)]
    current = parts[0] + parts[1] + parts[2]
    flux = parts[3] + parts[4] + parts[5]
    level_sum = jnp.sum(sheet[...], axis=0)
    level_rows = jnp.concatenate(
        [level_sum[i : i + 1, span] for i in range(lat_rows) for span in blocks_of(blocks)], 0
    )
    both = jnp.concatenate([current, flux + level_rows], 0)
    for k in range(sums.shape[0] // (2 * rows)):
        sums[k * 2 * rows : (k + 1) * 2 * rows] = both


def invert_kernel(arrived, lists, found, *, lat_rows):
    lon = lists.shape[1]
    blocks = lon // LANES
    owner = jnp.concatenate(
        [arrived[field_rows(OWNER, b, blocks), :] for b in range(blocks)], 1
    ).astype(jnp.int32)
    device = lax.broadcasted_iota(jnp.int32, owner.shape, 0)
    row = (owner >> 7) + device * (lat_rows * blocks) + 1
    lane = owner & (LANES - 1)
    cell = lists[...]
    cell_rows = found.shape[0] // 2
    found[...] = one_hot_sums(
        cell >> 7,
        cell & (LANES - 1),
        [row.astype(jnp.float32), lane.astype(jnp.float32)],
        cell_rows,
    ).astype(jnp.int32)


def advance_kernel(own, other, even, odd, advanced, window):
    theta_rows = advanced.shape[2]
    span = 4 * theta_rows
    is_odd = (lax.axis_index(RING) & 1) == 1
    window[...] = jnp.zeros_like(window)
    for shell, middle in enumerate((own, other)):
        for k in range(4):
            at = slice(k * theta_rows, (k + 1) * theta_rows)
            far = slice(shell * span + k * theta_rows, shell * span + (k + 1) * theta_rows)
            place = shell * 4 + k
            after = jnp.where(is_odd, odd[far], even[far])
            before = jnp.where(is_odd, even[far], odd[far])
            window[place, 0:theta_rows] = before
            window[place, theta_rows : 2 * theta_rows] = middle[at]
            window[place, 2 * theta_rows : 3 * theta_rows] = after
    rows, lon = window.shape[1:]
    spreading = [window[3], window[7]]
    for k in range(3):
        state = [window[k], window[4 + k]]
        for _ in range(DIFF_STEPS):
            later = []
            for shell in range(2):
                here = state[shell]
                around = state[1 - shell] + pltpu.roll(here, rows - 1, 0) + pltpu.roll(here, 1, 0)
                around = around + pltpu.roll(here, lon - 1, 1) + pltpu.roll(here, 1, 1)
                later.append(here + spreading[shell] * (around - 6.0 * here))
            state = later
        advanced[k, 0] = state[0][theta_rows : 2 * theta_rows]


def solve_kernel(sums, arrived, found, boundary, potential):
    lon = potential.shape[1]
    blocks = lon // LANES
    rows = 2 * blocks
    ring = lax.broadcasted_iota(jnp.int32, (PEERS, lon), 0)

    def summed(term, lat):
        return jnp.concatenate(
            [
                sum(
                    sums[pl.ds((pair * 2 + term) * rows + lat * blocks + b, PEERS, stride=4 * rows), :]
                    for pair in range(2)
                )
                for b in range(blocks)
            ],
            1,
        )

    def decay_rows(lat):
        return jnp.concatenate(
            [arrived[field_rows(DECAY + lat, b, blocks), :] for b in range(blocks)], 1
        )

    def before(values):
        return jnp.where(ring == 0, 0.0, pltpu.roll(values, 1, 0))

    def after(values):
        return jnp.where(ring == PEERS - 1, 0.0, pltpu.roll(values, PEERS - 1, 0))

    def east(values):
        return pltpu.roll(values, lon - 1, 1)

    def west(values):
        return pltpu.roll(values, 1, 1)

    aligned = [summed(0, 0), summed(0, 1)]
    conductance = [summed(1, 0), summed(1, 1)]
    faces = []
    middle = 0.5 * (conductance[0] + conductance[1])
    north = (0.5 * (conductance[0] + before(conductance[1])), middle)
    south = (middle, 0.5 * (conductance[1] + after(conductance[0])))
    level = []
    for lat in range(2):
        here = conductance[lat]
        east_face = 0.5 * (here + east(here))
        west_face = 0.5 * (here + west(here))
        diagonal = decay_rows(lat) + north[lat] + south[lat] + east_face + west_face
        inverse = 1.0 / diagonal
        faces.append([f * inverse for f in (north[lat], south[lat], east_face, west_face)])
        aligned[lat] = aligned[lat] * inverse
        level.append(aligned[lat])
    for _ in range(SWEEPS - 1):
        around = ((before(level[1]), level[1]), (level[0], after(level[0])))
        level = [
            aligned[lat]
            + faces[lat][0] * around[lat][0]
            + faces[lat][1] * around[lat][1]
            + faces[lat][2] * east(level[lat])
            + faces[lat][3] * west(level[lat])
            for lat in range(2)
        ]
    me = lax.axis_index(RING)
    for lat in range(2):
        potential[lat : lat + 1] = jnp.sum(
            jnp.where(ring == me, level[lat], 0.0), axis=0, keepdims=True
        )
    cell_rows = found.shape[0] // 2
    lane = found[cell_rows:]
    row = found[:cell_rows]
    taken = [jnp.zeros(lane.shape, jnp.float32)] * 2
    for device in range(PEERS):
        for lat in range(2):
            for b, span in enumerate(blocks_of(blocks)):
                here = row == device * rows + lat * blocks + b + 1
                for k, table in enumerate((level[lat], conductance[lat])):
                    one = table[device : device + 1, span]
                    taken[k] = jnp.where(here, pick_lanes(one, lane), taken[k])
    for k in range(2):
        for r in range(cell_rows):
            boundary[k, 0, r // blocks : r // blocks + 1, blocks_of(blocks)[r % blocks]] = taken[k][
                r : r + 1
            ]


def shape_of(*dims):
    return jax.ShapeDtypeStruct(dims, jnp.float32)


def short_plan(
    induction_vector,
    ohmic_spreading_number,
    reciprocal_surface,
    number_per_volume,
    thermal_kelvin,
    mapped_brick_members,
    arrival_owner_map,
    pedersen_sheet,
    electric_decay_rate,
):
    lists = mapped_brick_members[0, 0]
    owners = arrival_owner_map[0, 0]
    lat_rows, lon = electric_decay_rate.shape
    blocks = lon // LANES
    theta_rows = reciprocal_surface.shape[1]
    chunk_rows = CHUNK_FIELDS * blocks
    sent, field_packet = pl.pallas_call(
        collect_kernel,
        out_shape=(shape_of(PEERS * chunk_rows, LANES), shape_of(3 * theta_rows, lon)),
        name="collect",
    )(
        induction_vector,
        reciprocal_surface,
        number_per_volume,
        thermal_kelvin,
        lists,
        owners,
        electric_decay_rate,
    )
    arrived = lax.all_to_all(
        sent.reshape(PEERS, chunk_rows, LANES), RING, split_axis=0, concat_axis=0, tiled=True
    ).reshape(PEERS * chunk_rows, LANES)
    packet = jnp.concatenate([field_packet, ohmic_spreading_number[0]], 0)
    other = lax.ppermute(packet, "pair", [(0, 1), (1, 0)])
    both = jnp.concatenate([packet, other], 0)
    even = lax.ppermute(both, RING, [(i, i ^ 1) for i in range(PEERS)])
    odd_pairs = [(i, i + 1) for i in range(1, PEERS - 1, 2)]
    odd = lax.ppermute(both, RING, odd_pairs + [(j, i) for i, j in odd_pairs])
    copies = 2 * PEERS
    sum_rows = 2 * lat_rows * blocks
    sums = pl.pallas_call(
        deposit_kernel,
        out_shape=shape_of(copies * sum_rows, LANES),
        name="deposit",
    )(arrived, owners, pedersen_sheet)
    gathered = lax.all_to_all(
        sums.reshape(copies, sum_rows, LANES), GROUP, split_axis=0, concat_axis=0, tiled=True
    ).reshape(copies * sum_rows, LANES)
    found = pl.pallas_call(
        functools.partial(invert_kernel, lat_rows=lat_rows),
        out_shape=jax.ShapeDtypeStruct((2 * theta_rows * blocks, LANES), jnp.int32),
        name="invert",
    )(arrived, lists)
    advanced = pl.pallas_call(
        advance_kernel,
        out_shape=shape_of(3, 1, theta_rows, lon),
        scratch_shapes=[pltpu.VMEM((8, 4 * theta_rows, lon), jnp.float32)],
        name="advance",
    )(packet, other, even, odd)
    boundary, potential = pl.pallas_call(
        solve_kernel,
        out_shape=(shape_of(2, 1, theta_rows, lon), shape_of(lat_rows, lon)),
        name="solve",
    )(gathered, arrived, found)
    return advanced, boundary, potential


def local(*arguments):
    lists, decay, surface = arguments[5], arguments[8], arguments[2]
    fits = (
        lists.shape[2:] == (PEERS, decay.shape[1])
        and decay.shape == (2, 4 * LANES)
        and surface.shape == (1, 4, 4 * LANES)
        and lax.axis_size("pair") == 2
    )
    return short_plan(*arguments) if fits else stepwise(*arguments)


def solution(mesh):
    in_specs = (
        P(None, ("run", "pair"), ("tile", "sub"), None),
        P(("run", "pair"), ("tile", "sub"), None),
        P(("run", "pair"), ("tile", "sub"), None),
        P(("run", "pair"), ("tile", "sub"), None),
        P(("run", "pair"), ("tile", "sub"), None),
        P(("run", "pair"), ("tile", "sub"), None, None),
        P(("run", "pair"), ("tile", "sub"), None, None),
        P(("run", "pair"), ("tile", "sub"), None),
        P(("run", "tile", "sub"), None),
    )
    out_specs = (
        P(None, ("run", "pair"), ("tile", "sub"), None),
        P(None, ("run", "pair"), ("tile", "sub"), None),
        P(("run", "tile", "sub"), None),
    )
    return jax.shard_map(local, mesh=mesh, in_specs=in_specs, out_specs=out_specs, check_vma=False)
```

```python
import functools

import jax
import jax.numpy as jnp
from jax import lax
from jax.experimental import pallas as pl
from jax.experimental.pallas import tpu as pltpu
from jax.sharding import PartitionSpec as P

DIFF_STEPS = 4
SWEEPS = 8


def extended(cells, sides, width):
    for axis, dim in sides:
        count = lax.axis_size(axis)
        ends = count - 1
        head = lax.slice_in_dim(cells, 0, width, axis=dim)
        tail = lax.slice_in_dim(cells, cells.shape[dim] - width, cells.shape[dim], axis=dim)
        cells = jnp.concatenate(
            [
                lax.ppermute(tail, axis, [(i, (i + 1) % count) for i in range(ends)]),
                cells,
                lax.ppermute(head, axis, [((i + 1) % count, i) for i in range(ends)]),
            ],
            axis=dim,
        )
    return cells


def extend_cells(current_state):
    return extended(current_state, ((("tile", "sub"), 2), ("pair", 1)), 1)


def extend_columns(grid_values):
    return extended(grid_values, ((("tile", "sub"), 0),), 1)


def advance_field(current_state, padded, ohmic_spreading_number):
    neighbours = (
        padded[:, 2:, 1:-1] + padded[:, :-2, 1:-1] + padded[:, 1:-1, 2:] + padded[:, 1:-1, :-2]
    )
    neighbours = neighbours + jnp.roll(current_state, -1, 3) + jnp.roll(current_state, 1, 3)
    return current_state + ohmic_spreading_number * (neighbours - 6.0 * current_state)


def stepwise(
    induction_vector,
    ohmic_spreading_number,
    reciprocal_surface,
    number_per_volume,
    thermal_kelvin,
    mapped_brick_members,
    arrival_owner_map,
    pedersen_sheet,
    electric_decay_rate,
):
    padded = extend_cells(induction_vector)
    theta_diff = padded[2, 1:-1, 2:] - padded[2, 1:-1, :-2]
    phi_diff = jnp.roll(induction_vector[1], -1, 2) - jnp.roll(induction_vector[1], 1, 2)
    current = 0.5 * reciprocal_surface * (theta_diff - phi_diff)
    precipitation_power = 0.25 * number_per_volume * jnp.sqrt(thermal_kelvin)
    cell_lists = mapped_brick_members[0, 0]
    is_listed = cell_lists >= 0
    safe_index = jnp.where(is_listed, cell_lists, 0)
    sources = jnp.stack([current.reshape(-1), precipitation_power.reshape(-1)])
    payload = jnp.where(is_listed[None], sources[:, safe_index], 0.0)
    arrived = lax.all_to_all(payload, ("tile", "sub"), split_axis=1, concat_axis=1, tiled=True)
    land_columns = arrival_owner_map[0, 0]
    lat_rows, lon_cells = electric_decay_rate.shape
    column_count = lat_rows * lon_cells
    column_terms = (
        jnp.zeros((2, column_count), jnp.float32)
        .at[:, land_columns.reshape(-1)]
        .add(arrived.reshape(2, -1))
    )
    local_conductance = jnp.sum(pedersen_sheet, axis=0) + column_terms[1].reshape(
        lat_rows, lon_cells
    )
    aligned_current, conductance = lax.psum(
        (column_terms[0].reshape(lat_rows, lon_cells), local_conductance), "pair"
    )
    advanced = advance_field(induction_vector, padded, ohmic_spreading_number)
    for step_index in range(1, DIFF_STEPS):
        advanced = advance_field(advanced, extend_cells(advanced), ohmic_spreading_number)
    cond_rim = extend_columns(conductance)
    north_face = 0.5 * (conductance + cond_rim[:-2])
    south_face = 0.5 * (conductance + cond_rim[2:])
    east_face = 0.5 * (conductance + jnp.roll(conductance, -1, 1))
    west_face = 0.5 * (conductance + jnp.roll(conductance, 1, 1))
    diagonal = electric_decay_rate + north_face + south_face + east_face + west_face
    potential = aligned_current / diagonal
    for sweep_index in range(SWEEPS - 1):
        potential_rim = extend_columns(potential)
        potential = (
            aligned_current
            + north_face * potential_rim[:-2]
            + south_face * potential_rim[2:]
            + east_face * jnp.roll(potential, -1, 1)
            + west_face * jnp.roll(potential, 1, 1)
        ) / diagonal
    column_values = jnp.stack([potential, conductance]).reshape(2, -1)
    returned = lax.all_to_all(
        column_values[:, land_columns], ("tile", "sub"), split_axis=1, concat_axis=1, tiled=True
    )
    cell_count = current.size
    target = jnp.where(is_listed, cell_lists, cell_count)
    boundary = jnp.zeros((2, cell_count), jnp.float32).at[:, target].add(returned, mode="drop")
    boundary = boundary.reshape((2,) + current.shape)
    return (advanced, boundary, potential)


LANES = 128
PEERS = 8
RING = ("tile", "sub")
GROUP = ("tile", "sub", "pair")
CURRENT, FLUX, RIM_WEIGHT, CELL, OWNER, FIRST_ROW, LAST_ROW, DECAY = range(8)
CHUNK_FIELDS = 10
KERNEL_PARAMS = pltpu.CompilerParams(vmem_limit_bytes=4 * 2**20)


def pick_lanes(row, lane):
    return jnp.take_along_axis(
        jnp.broadcast_to(row, lane.shape), lane, axis=1, mode="promise_in_bounds"
    )


def blocks_of(count):
    return [slice(b * LANES, (b + 1) * LANES) for b in range(count)]


def field_rows(field, block, blocks):
    return pl.ds(field * blocks + block, PEERS, stride=CHUNK_FIELDS * blocks)


def three_terms(values):
    first = values.astype(jnp.bfloat16)
    rest = values - first.astype(jnp.float32)
    second = rest.astype(jnp.bfloat16)
    third = (rest - second.astype(jnp.float32)).astype(jnp.bfloat16)
    return first, second, third


def one_hot_sums(rows, lanes, terms, row_count):
    total = None
    slots = rows.shape[1]
    row_at = lax.broadcasted_iota(jnp.int32, (row_count, slots), 0)
    lane_at = lax.broadcasted_iota(jnp.int32, (LANES, slots), 0)
    for s in range(rows.shape[0]):
        here = row_at == rows[s : s + 1]
        left = jnp.concatenate(
            [
                jnp.where(here, jnp.broadcast_to(t[s : s + 1], here.shape), 0.0)
                for t in terms
            ],
            axis=0,
        ).astype(jnp.bfloat16)
        right = jnp.where(lane_at == lanes[s : s + 1], 1.0, 0.0).astype(jnp.bfloat16)
        part = lax.dot_general(
            left, right, (((1,), (1,)), ((), ())), preferred_element_type=jnp.float32
        )
        total = part if total is None else total + part
    return total


def collect_kernel(*refs):
    count = 8
    here, (sent, packet), mine, (arrival,) = (
        refs[:count],
        refs[count : count + 2],
        refs[count + 2 : 2 * count + 2],
        refs[2 * count + 2 :],
    )
    copies = [pltpu.make_async_copy(here[k], mine[k], arrival.at[k]) for k in range(count)]
    for copy in copies:
        copy.start()
    for copy in copies:
        copy.wait()
    field, reciprocal, number, kelvin, lists, owners, decay, spreading = mine
    theta_rows, lon = reciprocal.shape[1:]
    blocks = lon // LANES
    toward_theta = field[2, 0]
    toward_phi = field[1, 0]
    zero_row = jnp.zeros((1, lon), jnp.float32)
    half = 0.5 * reciprocal[0]
    theta_diff = jnp.concatenate([toward_theta[1:], zero_row], 0) - jnp.concatenate(
        [zero_row, toward_theta[:-1]], 0
    )
    phi_diff = pltpu.roll(toward_phi, lon - 1, 1) - pltpu.roll(toward_phi, 1, 1)
    current = half * (theta_diff - phi_diff)
    flux = 0.25 * number[0] * jnp.sqrt(kelvin[0])
    for b, span in enumerate(blocks_of(blocks)):
        cell = lists[:, span]
        lane = cell & (LANES - 1)
        row = cell >> 7
        taken = [jnp.zeros(cell.shape, jnp.float32)] * 3
        for theta in range(theta_rows):
            for c, source in enumerate(blocks_of(blocks)):
                here = row == theta * blocks + c
                at = slice(theta, theta + 1)
                tables = [current[at, source], flux[at, source]]
                if theta == 0:
                    tables.append(-half[at, source])
                if theta == theta_rows - 1:
                    tables.append(half[at, source])
                for k, table in enumerate(tables):
                    taken[k] = jnp.where(here, pick_lanes(table, lane), taken[k])
        values = taken + [cell.astype(jnp.float32), owners[:, span].astype(jnp.float32)]
        values += [
            jnp.broadcast_to(r[:, span], cell.shape)
            for r in (toward_theta[:1], toward_theta[-1:], decay[0:1], decay[1:2])
        ]
        values.append(jnp.zeros(cell.shape, jnp.float32))
        for k, value in enumerate(values):
            sent[field_rows(k, b, blocks), :] = value
    for k in range(3):
        packet[k * theta_rows : (k + 1) * theta_rows] = field[k, 0]
    packet[3 * theta_rows : 4 * theta_rows] = spreading[0]


def deposit_kernel(arrived, owners, sheet, sums):
    lon = sheet.shape[-1]
    blocks = lon // LANES
    lat_rows = sheet.shape[1]
    peer = lax.broadcasted_iota(jnp.int32, (PEERS, LANES), 0)
    above, below = [], []
    for b in range(blocks):
        last = pltpu.roll(arrived[field_rows(LAST_ROW, b, blocks), :], 1, 0)
        above.append(jnp.where(peer == 0, 0.0, last))
        first = pltpu.roll(arrived[field_rows(FIRST_ROW, b, blocks), :], PEERS - 1, 0)
        below.append(jnp.where(peer == PEERS - 1, 0.0, first))
    currents, fluxes = [], []
    for b in range(blocks):
        cell = arrived[field_rows(CELL, b, blocks), :].astype(jnp.int32)
        phi_block = (cell >> 7) & (blocks - 1)
        lane = cell & (LANES - 1)
        rim = jnp.zeros((PEERS, LANES), jnp.float32)
        for c in range(blocks):
            found = jnp.where(
                cell < lon, pick_lanes(above[c], lane), pick_lanes(below[c], lane)
            )
            rim = jnp.where(phi_block == c, found, rim)
        weight = arrived[field_rows(RIM_WEIGHT, b, blocks), :]
        currents.append(arrived[field_rows(CURRENT, b, blocks), :] + weight * rim)
        fluxes.append(arrived[field_rows(FLUX, b, blocks), :])
    column = owners[...]
    terms = three_terms(jnp.concatenate(currents, 1)) + three_terms(jnp.concatenate(fluxes, 1))
    rows = lat_rows * blocks
    total = one_hot_sums(
        column >> 7, column & (LANES - 1), [t.astype(jnp.float32) for t in terms], rows
    )
    parts = [total[k * rows : (k + 1) * rows] for k in range(6)]
    current = parts[0] + parts[1] + parts[2]
    flux = parts[3] + parts[4] + parts[5]
    level_sum = jnp.sum(sheet[...], axis=0)
    level_rows = jnp.concatenate(
        [level_sum[i : i + 1, span] for i in range(lat_rows) for span in blocks_of(blocks)], 0
    )
    both = jnp.concatenate([current, flux + level_rows], 0)
    for k in range(sums.shape[0] // (2 * rows)):
        sums[k * 2 * rows : (k + 1) * 2 * rows] = both


def invert_kernel(arrived, lists, found, *, lat_rows):
    lon = lists.shape[1]
    blocks = lon // LANES
    owner = jnp.concatenate(
        [arrived[field_rows(OWNER, b, blocks), :] for b in range(blocks)], 1
    ).astype(jnp.int32)
    device = lax.broadcasted_iota(jnp.int32, owner.shape, 0)
    row = (owner >> 7) + device * (lat_rows * blocks) + 1
    lane = owner & (LANES - 1)
    cell = lists[...]
    cell_rows = found.shape[0] // 2
    found[...] = one_hot_sums(
        cell >> 7,
        cell & (LANES - 1),
        [row.astype(jnp.float32), lane.astype(jnp.float32)],
        cell_rows,
    ).astype(jnp.int32)


def advance_kernel(own, other, even, odd, advanced, window):
    theta_rows = advanced.shape[2]
    span = 4 * theta_rows
    is_odd = (lax.axis_index(RING) & 1) == 1
    window[...] = jnp.zeros_like(window)
    for shell, middle in enumerate((own, other)):
        for k in range(4):
            at = slice(k * theta_rows, (k + 1) * theta_rows)
            far = slice(shell * span + k * theta_rows, shell * span + (k + 1) * theta_rows)
            place = shell * 4 + k
            after = jnp.where(is_odd, odd[far], even[far])
            before = jnp.where(is_odd, even[far], odd[far])
            window[place, 0:theta_rows] = before
            window[place, theta_rows : 2 * theta_rows] = middle[at]
            window[place, 2 * theta_rows : 3 * theta_rows] = after
    rows, lon = window.shape[1:]
    spreading = [window[3], window[7]]
    for k in range(3):
        state = [window[k], window[4 + k]]
        for _ in range(DIFF_STEPS):
            later = []
            for shell in range(2):
                here = state[shell]
                around = state[1 - shell] + pltpu.roll(here, rows - 1, 0) + pltpu.roll(here, 1, 0)
                around = around + pltpu.roll(here, lon - 1, 1) + pltpu.roll(here, 1, 1)
                later.append(here + spreading[shell] * (around - 6.0 * here))
            state = later
        advanced[k, 0] = state[0][theta_rows : 2 * theta_rows]


def solve_kernel(sums, arrived, found, boundary, potential):
    lon = potential.shape[1]
    blocks = lon // LANES
    rows = 2 * blocks
    ring = lax.broadcasted_iota(jnp.int32, (PEERS, lon), 0)

    def summed(term, lat):
        return jnp.concatenate(
            [
                sum(
                    sums[pl.ds((pair * 2 + term) * rows + lat * blocks + b, PEERS, stride=4 * rows), :]
                    for pair in range(2)
                )
                for b in range(blocks)
            ],
            1,
        )

    def decay_rows(lat):
        return jnp.concatenate(
            [arrived[field_rows(DECAY + lat, b, blocks), :] for b in range(blocks)], 1
        )

    def before(values):
        return jnp.where(ring == 0, 0.0, pltpu.roll(values, 1, 0))

    def after(values):
        return jnp.where(ring == PEERS - 1, 0.0, pltpu.roll(values, PEERS - 1, 0))

    def east(values):
        return pltpu.roll(values, lon - 1, 1)

    def west(values):
        return pltpu.roll(values, 1, 1)

    aligned = [summed(0, 0), summed(0, 1)]
    conductance = [summed(1, 0), summed(1, 1)]
    faces = []
    middle = 0.5 * (conductance[0] + conductance[1])
    north = (0.5 * (conductance[0] + before(conductance[1])), middle)
    south = (middle, 0.5 * (conductance[1] + after(conductance[0])))
    level = []
    for lat in range(2):
        here = conductance[lat]
        east_face = 0.5 * (here + east(here))
        west_face = 0.5 * (here + west(here))
        diagonal = decay_rows(lat) + north[lat] + south[lat] + east_face + west_face
        inverse = 1.0 / diagonal
        faces.append([f * inverse for f in (north[lat], south[lat], east_face, west_face)])
        aligned[lat] = aligned[lat] * inverse
        level.append(aligned[lat])
    for _ in range(SWEEPS - 1):
        around = ((before(level[1]), level[1]), (level[0], after(level[0])))
        level = [
            aligned[lat]
            + faces[lat][0] * around[lat][0]
            + faces[lat][1] * around[lat][1]
            + faces[lat][2] * east(level[lat])
            + faces[lat][3] * west(level[lat])
            for lat in range(2)
        ]
    me = lax.axis_index(RING)
    for lat in range(2):
        potential[lat : lat + 1] = jnp.sum(
            jnp.where(ring == me, level[lat], 0.0), axis=0, keepdims=True
        )
    cell_rows = found.shape[0] // 2
    lane = found[cell_rows:]
    row = found[:cell_rows]
    taken = [jnp.zeros(lane.shape, jnp.float32)] * 2
    for device in range(PEERS):
        for lat in range(2):
            for b, span in enumerate(blocks_of(blocks)):
                here = row == device * rows + lat * blocks + b + 1
                for k, table in enumerate((level[lat], conductance[lat])):
                    one = table[device : device + 1, span]
                    taken[k] = jnp.where(here, pick_lanes(one, lane), taken[k])
    for k in range(2):
        for r in range(cell_rows):
            boundary[k, 0, r // blocks : r // blocks + 1, blocks_of(blocks)[r % blocks]] = taken[k][
                r : r + 1
            ]


def shape_of(*dims):
    return jax.ShapeDtypeStruct(dims, jnp.float32)


def short_plan(
    induction_vector,
    ohmic_spreading_number,
    reciprocal_surface,
    number_per_volume,
    thermal_kelvin,
    mapped_brick_members,
    arrival_owner_map,
    pedersen_sheet,
    electric_decay_rate,
):
    lists = mapped_brick_members[0, 0]
    owners = arrival_owner_map[0, 0]
    lat_rows, lon = electric_decay_rate.shape
    blocks = lon // LANES
    theta_rows = reciprocal_surface.shape[1]
    chunk_rows = CHUNK_FIELDS * blocks
    arguments = (
        induction_vector,
        reciprocal_surface,
        number_per_volume,
        thermal_kelvin,
        lists,
        owners,
        electric_decay_rate,
        ohmic_spreading_number,
    )
    sent, packet = pl.pallas_call(
        collect_kernel,
        out_shape=(shape_of(PEERS * chunk_rows, LANES), shape_of(4 * theta_rows, lon)),
        in_specs=[pl.BlockSpec(memory_space=pltpu.HBM)] * len(arguments),
        scratch_shapes=[pltpu.VMEM(a.shape, a.dtype) for a in arguments]
        + [pltpu.SemaphoreType.DMA((len(arguments),))],
        compiler_params=KERNEL_PARAMS,
        name="collect",
    )(*[pltpu.with_memory_space_constraint(a, pltpu.HBM) for a in arguments])
    arrived = lax.all_to_all(
        sent.reshape(PEERS, chunk_rows, LANES), RING, split_axis=0, concat_axis=0, tiled=True
    ).reshape(PEERS * chunk_rows, LANES)
    other = lax.ppermute(packet, "pair", [(0, 1), (1, 0)])
    both = jnp.concatenate([packet, other], 0)
    even = lax.ppermute(both, RING, [(i, i ^ 1) for i in range(PEERS)])
    arrived, both, even = lax.optimization_barrier((arrived, both, even))
    odd_pairs = [(i, i + 1) for i in range(1, PEERS - 1, 2)]
    odd = lax.ppermute(both, RING, odd_pairs + [(j, i) for i, j in odd_pairs])
    copies = 2 * PEERS
    sum_rows = 2 * lat_rows * blocks
    sums = pl.pallas_call(
        deposit_kernel,
        out_shape=shape_of(copies * sum_rows, LANES),
        compiler_params=KERNEL_PARAMS,
        name="deposit",
    )(arrived, owners, pedersen_sheet)
    gathered = lax.all_to_all(
        sums.reshape(copies, sum_rows, LANES), GROUP, split_axis=0, concat_axis=0, tiled=True
    ).reshape(copies * sum_rows, LANES)
    found = pl.pallas_call(
        functools.partial(invert_kernel, lat_rows=lat_rows),
        out_shape=jax.ShapeDtypeStruct((2 * theta_rows * blocks, LANES), jnp.int32),
        compiler_params=KERNEL_PARAMS,
        name="invert",
    )(arrived, lists)
    advanced = pl.pallas_call(
        advance_kernel,
        out_shape=shape_of(3, 1, theta_rows, lon),
        scratch_shapes=[pltpu.VMEM((8, 4 * theta_rows, lon), jnp.float32)],
        compiler_params=KERNEL_PARAMS,
        name="advance",
    )(packet, other, even, odd)
    boundary, potential = pl.pallas_call(
        solve_kernel,
        out_shape=(shape_of(2, 1, theta_rows, lon), shape_of(lat_rows, lon)),
        compiler_params=KERNEL_PARAMS,
        name="solve",
    )(gathered, arrived, found)
    return advanced, boundary, potential


def local(*arguments):
    lists, decay, surface = arguments[5], arguments[8], arguments[2]
    fits = (
        lists.shape[2:] == (PEERS, decay.shape[1])
        and decay.shape == (2, 4 * LANES)
        and surface.shape == (1, 4, 4 * LANES)
        and lax.axis_size("pair") == 2
    )
    return short_plan(*arguments) if fits else stepwise(*arguments)


def solution(mesh):
    in_specs = (
        P(None, ("run", "pair"), ("tile", "sub"), None),
        P(("run", "pair"), ("tile", "sub"), None),
        P(("run", "pair"), ("tile", "sub"), None),
        P(("run", "pair"), ("tile", "sub"), None),
        P(("run", "pair"), ("tile", "sub"), None),
        P(("run", "pair"), ("tile", "sub"), None, None),
        P(("run", "pair"), ("tile", "sub"), None, None),
        P(("run", "pair"), ("tile", "sub"), None),
        P(("run", "tile", "sub"), None),
    )
    out_specs = (
        P(None, ("run", "pair"), ("tile", "sub"), None),
        P(None, ("run", "pair"), ("tile", "sub"), None),
        P(("run", "tile", "sub"), None),
    )
    return jax.shard_map(local, mesh=mesh, in_specs=in_specs, out_specs=out_specs, check_vma=False)
```

```python
import functools

import jax
import jax.numpy as jnp
from jax import lax
from jax.experimental import pallas as pl
from jax.experimental.pallas import tpu as pltpu
from jax.sharding import PartitionSpec as P

DIFF_STEPS = 4
SWEEPS = 8


def extended(cells, sides, width):
    for axis, dim in sides:
        count = lax.axis_size(axis)
        ends = count - 1
        head = lax.slice_in_dim(cells, 0, width, axis=dim)
        tail = lax.slice_in_dim(cells, cells.shape[dim] - width, cells.shape[dim], axis=dim)
        cells = jnp.concatenate(
            [
                lax.ppermute(tail, axis, [(i, (i + 1) % count) for i in range(ends)]),
                cells,
                lax.ppermute(head, axis, [((i + 1) % count, i) for i in range(ends)]),
            ],
            axis=dim,
        )
    return cells


def extend_cells(current_state):
    return extended(current_state, ((("tile", "sub"), 2), ("pair", 1)), 1)


def extend_columns(grid_values):
    return extended(grid_values, ((("tile", "sub"), 0),), 1)


def advance_field(current_state, padded, ohmic_spreading_number):
    neighbours = (
        padded[:, 2:, 1:-1] + padded[:, :-2, 1:-1] + padded[:, 1:-1, 2:] + padded[:, 1:-1, :-2]
    )
    neighbours = neighbours + jnp.roll(current_state, -1, 3) + jnp.roll(current_state, 1, 3)
    return current_state + ohmic_spreading_number * (neighbours - 6.0 * current_state)


def stepwise(
    induction_vector,
    ohmic_spreading_number,
    reciprocal_surface,
    number_per_volume,
    thermal_kelvin,
    mapped_brick_members,
    arrival_owner_map,
    pedersen_sheet,
    electric_decay_rate,
):
    padded = extend_cells(induction_vector)
    theta_diff = padded[2, 1:-1, 2:] - padded[2, 1:-1, :-2]
    phi_diff = jnp.roll(induction_vector[1], -1, 2) - jnp.roll(induction_vector[1], 1, 2)
    current = 0.5 * reciprocal_surface * (theta_diff - phi_diff)
    precipitation_power = 0.25 * number_per_volume * jnp.sqrt(thermal_kelvin)
    cell_lists = mapped_brick_members[0, 0]
    is_listed = cell_lists >= 0
    safe_index = jnp.where(is_listed, cell_lists, 0)
    sources = jnp.stack([current.reshape(-1), precipitation_power.reshape(-1)])
    payload = jnp.where(is_listed[None], sources[:, safe_index], 0.0)
    arrived = lax.all_to_all(payload, ("tile", "sub"), split_axis=1, concat_axis=1, tiled=True)
    land_columns = arrival_owner_map[0, 0]
    lat_rows, lon_cells = electric_decay_rate.shape
    column_count = lat_rows * lon_cells
    column_terms = (
        jnp.zeros((2, column_count), jnp.float32)
        .at[:, land_columns.reshape(-1)]
        .add(arrived.reshape(2, -1))
    )
    local_conductance = jnp.sum(pedersen_sheet, axis=0) + column_terms[1].reshape(
        lat_rows, lon_cells
    )
    aligned_current, conductance = lax.psum(
        (column_terms[0].reshape(lat_rows, lon_cells), local_conductance), "pair"
    )
    advanced = advance_field(induction_vector, padded, ohmic_spreading_number)
    for step_index in range(1, DIFF_STEPS):
        advanced = advance_field(advanced, extend_cells(advanced), ohmic_spreading_number)
    cond_rim = extend_columns(conductance)
    north_face = 0.5 * (conductance + cond_rim[:-2])
    south_face = 0.5 * (conductance + cond_rim[2:])
    east_face = 0.5 * (conductance + jnp.roll(conductance, -1, 1))
    west_face = 0.5 * (conductance + jnp.roll(conductance, 1, 1))
    diagonal = electric_decay_rate + north_face + south_face + east_face + west_face
    potential = aligned_current / diagonal
    for sweep_index in range(SWEEPS - 1):
        potential_rim = extend_columns(potential)
        potential = (
            aligned_current
            + north_face * potential_rim[:-2]
            + south_face * potential_rim[2:]
            + east_face * jnp.roll(potential, -1, 1)
            + west_face * jnp.roll(potential, 1, 1)
        ) / diagonal
    column_values = jnp.stack([potential, conductance]).reshape(2, -1)
    returned = lax.all_to_all(
        column_values[:, land_columns], ("tile", "sub"), split_axis=1, concat_axis=1, tiled=True
    )
    cell_count = current.size
    target = jnp.where(is_listed, cell_lists, cell_count)
    boundary = jnp.zeros((2, cell_count), jnp.float32).at[:, target].add(returned, mode="drop")
    boundary = boundary.reshape((2,) + current.shape)
    return (advanced, boundary, potential)


LANES = 128
PEERS = 8
RING = ("tile", "sub")
GROUP = ("tile", "sub", "pair")
CURRENT, FLUX, RIM_WEIGHT, CELL, OWNER, FIRST_ROW, LAST_ROW, DECAY = range(8)
CHUNK_FIELDS = 10
KERNEL_PARAMS = pltpu.CompilerParams(vmem_limit_bytes=4 * 2**20)


SLOT_ORDER = [5, 4, 3, 2, 1, 0, 7, 6]
SUM_ORDER = [5, 4, 3, 2, 1, 0, 7, 6]
SUM_PAIRS = (1, 0)


def by_position(values, width=LANES):
    row = lax.broadcasted_iota(jnp.int32, (PEERS, width), 0)
    out = jnp.zeros((PEERS, width), jnp.int32)
    for k, value in enumerate(values):
        out = jnp.where(row == k, value, out)
    return out


def take_rows(values, index):
    return jnp.take_along_axis(values, index, axis=0, mode="promise_in_bounds")


def neighbour_rows(values, order, step):
    wanted = [d + step for d in order]
    inside = [0 <= d < PEERS for d in wanted]
    index = by_position([order.index(d) if ok else 0 for d, ok in zip(wanted, inside)])
    valid = by_position([int(ok) for ok in inside]) == 1
    columns = blocks_of(values.shape[1] // LANES)
    return jnp.concatenate(
        [jnp.where(valid, take_rows(values[:, c], index), 0.0) for c in columns], 1
    )


def pick_lanes(row, lane):
    return jnp.take_along_axis(
        jnp.broadcast_to(row, lane.shape), lane, axis=1, mode="promise_in_bounds"
    )


def blocks_of(count):
    return [slice(b * LANES, (b + 1) * LANES) for b in range(count)]


def field_rows(field, block, blocks):
    return pl.ds(field * blocks + block, PEERS, stride=CHUNK_FIELDS * blocks)


def three_terms(values):
    first = values.astype(jnp.bfloat16)
    rest = values - first.astype(jnp.float32)
    second = rest.astype(jnp.bfloat16)
    third = (rest - second.astype(jnp.float32)).astype(jnp.bfloat16)
    return first, second, third


def one_hot_sums(rows, lanes, terms, row_count):
    total = None
    slots = rows.shape[1]
    row_at = lax.broadcasted_iota(jnp.int32, (row_count, slots), 0)
    lane_at = lax.broadcasted_iota(jnp.int32, (LANES, slots), 0)
    for s in range(rows.shape[0]):
        here = row_at == rows[s : s + 1]
        left = jnp.concatenate(
            [
                jnp.where(here, jnp.broadcast_to(t[s : s + 1], here.shape), 0.0)
                for t in terms
            ],
            axis=0,
        ).astype(jnp.bfloat16)
        right = jnp.where(lane_at == lanes[s : s + 1], 1.0, 0.0).astype(jnp.bfloat16)
        part = lax.dot_general(
            left, right, (((1,), (1,)), ((), ())), preferred_element_type=jnp.float32
        )
        total = part if total is None else total + part
    return total


def collect_kernel(*refs):
    count = 8
    here, (sent, packet), mine, (arrival,) = (
        refs[:count],
        refs[count : count + 2],
        refs[count + 2 : 2 * count + 2],
        refs[2 * count + 2 :],
    )
    copies = [pltpu.make_async_copy(here[k], mine[k], arrival.at[k]) for k in range(count)]
    for copy in copies:
        copy.start()
    for copy in copies:
        copy.wait()
    field, reciprocal, number, kelvin, lists, owners, decay, spreading = mine
    theta_rows, lon = reciprocal.shape[1:]
    blocks = lon // LANES
    toward_theta = field[2, 0]
    toward_phi = field[1, 0]
    zero_row = jnp.zeros((1, lon), jnp.float32)
    half = 0.5 * reciprocal[0]
    theta_diff = jnp.concatenate([toward_theta[1:], zero_row], 0) - jnp.concatenate(
        [zero_row, toward_theta[:-1]], 0
    )
    phi_diff = pltpu.roll(toward_phi, lon - 1, 1) - pltpu.roll(toward_phi, 1, 1)
    current = half * (theta_diff - phi_diff)
    flux = 0.25 * number[0] * jnp.sqrt(kelvin[0])
    order = by_position(SLOT_ORDER)
    for b, span in enumerate(blocks_of(blocks)):
        cell = take_rows(lists[:, span], order)
        lane = cell & (LANES - 1)
        row = cell >> 7
        taken = [jnp.zeros(cell.shape, jnp.float32)] * 3
        for theta in range(theta_rows):
            for c, source in enumerate(blocks_of(blocks)):
                here = row == theta * blocks + c
                at = slice(theta, theta + 1)
                tables = [current[at, source], flux[at, source]]
                if theta == 0:
                    tables.append(-half[at, source])
                if theta == theta_rows - 1:
                    tables.append(half[at, source])
                for k, table in enumerate(tables):
                    taken[k] = jnp.where(here, pick_lanes(table, lane), taken[k])
        values = taken + [cell.astype(jnp.float32), take_rows(owners[:, span], order).astype(jnp.float32)]
        values += [
            jnp.broadcast_to(r[:, span], cell.shape)
            for r in (toward_theta[:1], toward_theta[-1:], decay[0:1], decay[1:2])
        ]
        values.append(jnp.zeros(cell.shape, jnp.float32))
        for k, value in enumerate(values):
            sent[field_rows(k, b, blocks), :] = value
    for k in range(3):
        packet[k * theta_rows : (k + 1) * theta_rows] = field[k, 0]
    packet[3 * theta_rows : 4 * theta_rows] = spreading[0]


def deposit_kernel(arrived, owners, sheet, sums):
    lon = sheet.shape[-1]
    blocks = lon // LANES
    lat_rows = sheet.shape[1]
    above = [
        neighbour_rows(arrived[field_rows(LAST_ROW, b, blocks), :], SLOT_ORDER, -1) for b in range(blocks)
    ]
    below = [
        neighbour_rows(arrived[field_rows(FIRST_ROW, b, blocks), :], SLOT_ORDER, 1) for b in range(blocks)
    ]
    currents, fluxes = [], []
    for b in range(blocks):
        cell = arrived[field_rows(CELL, b, blocks), :].astype(jnp.int32)
        phi_block = (cell >> 7) & (blocks - 1)
        lane = cell & (LANES - 1)
        rim = jnp.zeros((PEERS, LANES), jnp.float32)
        for c in range(blocks):
            found = jnp.where(
                cell < lon, pick_lanes(above[c], lane), pick_lanes(below[c], lane)
            )
            rim = jnp.where(phi_block == c, found, rim)
        weight = arrived[field_rows(RIM_WEIGHT, b, blocks), :]
        currents.append(arrived[field_rows(CURRENT, b, blocks), :] + weight * rim)
        fluxes.append(arrived[field_rows(FLUX, b, blocks), :])
    order = by_position(SLOT_ORDER)
    column = jnp.concatenate(
        [take_rows(owners[:, span], order) for span in blocks_of(blocks)], 1
    )
    terms = three_terms(jnp.concatenate(currents, 1)) + three_terms(jnp.concatenate(fluxes, 1))
    rows = lat_rows * blocks
    total = one_hot_sums(
        column >> 7, column & (LANES - 1), [t.astype(jnp.float32) for t in terms], rows
    )
    parts = [total[k * rows : (k + 1) * rows] for k in range(6)]
    current = parts[0] + parts[1] + parts[2]
    flux = parts[3] + parts[4] + parts[5]
    level_sum = jnp.sum(sheet[...], axis=0)
    level_rows = jnp.concatenate(
        [level_sum[i : i + 1, span] for i in range(lat_rows) for span in blocks_of(blocks)], 0
    )
    both = jnp.concatenate([current, flux + level_rows], 0)
    for k in range(sums.shape[0] // (2 * rows)):
        sums[k * 2 * rows : (k + 1) * 2 * rows] = both


def footpoints(arrived, lists, lat_rows, cell_rows):
    lon = lists.shape[1]
    blocks = lon // LANES
    owner = jnp.concatenate(
        [arrived[field_rows(OWNER, b, blocks), :] for b in range(blocks)], 1
    ).astype(jnp.int32)
    device = by_position(SLOT_ORDER, lon)
    row = (owner >> 7) + device * (lat_rows * blocks) + 1
    lane = owner & (LANES - 1)
    order = by_position(SLOT_ORDER)
    cell = jnp.concatenate([take_rows(lists[:, span], order) for span in blocks_of(blocks)], 1)
    found = one_hot_sums(
        cell >> 7,
        cell & (LANES - 1),
        [row.astype(jnp.float32), lane.astype(jnp.float32)],
        cell_rows,
    ).astype(jnp.int32)
    return found[:cell_rows], found[cell_rows:]


def advance_body(own, other, even, odd, advanced, window):
    theta_rows = advanced.shape[2]
    span = 4 * theta_rows
    is_odd = (lax.axis_index(RING) & 1) == 1
    window[...] = jnp.zeros_like(window)
    for shell, middle in enumerate((own, other)):
        for k in range(4):
            at = slice(k * theta_rows, (k + 1) * theta_rows)
            far = slice(shell * span + k * theta_rows, shell * span + (k + 1) * theta_rows)
            place = shell * 4 + k
            window[place, 0:theta_rows] = jnp.where(is_odd, even[far], odd[far])
            window[place, theta_rows : 2 * theta_rows] = middle[at]
            window[place, 2 * theta_rows : 3 * theta_rows] = jnp.where(is_odd, odd[far], even[far])
    rows, lon = window.shape[1:]
    spreading = [window[3], window[7]]
    for k in range(3):
        state = [window[k], window[4 + k]]
        for _ in range(DIFF_STEPS):
            later = []
            for shell in range(2):
                here = state[shell]
                around = state[1 - shell] + pltpu.roll(here, rows - 1, 0) + pltpu.roll(here, 1, 0)
                around = around + pltpu.roll(here, lon - 1, 1) + pltpu.roll(here, 1, 1)
                later.append(here + spreading[shell] * (around - 6.0 * here))
            state = later
        advanced[k, 0] = state[0][theta_rows : 2 * theta_rows]


def solve_body(sums, arrived, lists, boundary, potential):
    lon = potential.shape[1]
    blocks = lon // LANES
    rows = 2 * blocks
    cell_rows = boundary.shape[2] * blocks
    row, lane = footpoints(arrived, lists, 2, cell_rows)
    ring = by_position(SUM_ORDER, lon)
    place_of = by_position([SLOT_ORDER.index(d) for d in SUM_ORDER])

    def summed(term, lat):
        return jnp.concatenate(
            [
                sum(
                    sums[pl.ds((pair * 2 + term) * rows + lat * blocks + b, PEERS, stride=4 * rows), :]
                    for pair in range(2)
                )
                for b in range(blocks)
            ],
            1,
        )

    def decay_rows(lat):
        return jnp.concatenate(
            [
                take_rows(arrived[field_rows(DECAY + lat, b, blocks), :], place_of)
                for b in range(blocks)
            ],
            1,
        )

    def before(values):
        return neighbour_rows(values, SUM_ORDER, -1)

    def after(values):
        return neighbour_rows(values, SUM_ORDER, 1)

    def east(values):
        return pltpu.roll(values, lon - 1, 1)

    def west(values):
        return pltpu.roll(values, 1, 1)

    aligned = [summed(0, 0), summed(0, 1)]
    conductance = [summed(1, 0), summed(1, 1)]
    faces = []
    middle = 0.5 * (conductance[0] + conductance[1])
    north = (0.5 * (conductance[0] + before(conductance[1])), middle)
    south = (middle, 0.5 * (conductance[1] + after(conductance[0])))
    level = []
    for lat in range(2):
        here = conductance[lat]
        east_face = 0.5 * (here + east(here))
        west_face = 0.5 * (here + west(here))
        diagonal = decay_rows(lat) + north[lat] + south[lat] + east_face + west_face
        inverse = 1.0 / diagonal
        faces.append([f * inverse for f in (north[lat], south[lat], east_face, west_face)])
        aligned[lat] = aligned[lat] * inverse
        level.append(aligned[lat])
    for _ in range(SWEEPS - 1):
        around = ((before(level[1]), level[1]), (level[0], after(level[0])))
        level = [
            aligned[lat]
            + faces[lat][0] * around[lat][0]
            + faces[lat][1] * around[lat][1]
            + faces[lat][2] * east(level[lat])
            + faces[lat][3] * west(level[lat])
            for lat in range(2)
        ]
    me = lax.axis_index(RING)
    for lat in range(2):
        potential[lat : lat + 1] = jnp.sum(
            jnp.where(ring == me, level[lat], 0.0), axis=0, keepdims=True
        )
    taken = [jnp.zeros(lane.shape, jnp.float32)] * 2
    for place, device in enumerate(SUM_ORDER):
        for lat in range(2):
            for b, span in enumerate(blocks_of(blocks)):
                here = row == device * rows + lat * blocks + b + 1
                for k, table in enumerate((level[lat], conductance[lat])):
                    one = table[place : place + 1, span]
                    taken[k] = jnp.where(here, pick_lanes(one, lane), taken[k])
    for k in range(2):
        for r in range(cell_rows):
            boundary[k, 0, r // blocks : r // blocks + 1, blocks_of(blocks)[r % blocks]] = taken[k][
                r : r + 1
            ]


def finish_kernel(
    sums, arrived, lists, own, other, even, odd, advanced, boundary, potential, window
):
    advance_body(own, other, even, odd, advanced, window)
    solve_body(sums, arrived, lists, boundary, potential)


def shape_of(*dims):
    return jax.ShapeDtypeStruct(dims, jnp.float32)


def exchange(chunks, axes, order):
    return lax.all_to_all(
        chunks, axes, split_axis=0, concat_axis=0, axis_index_groups=[order], tiled=True
    )


def short_plan(
    induction_vector,
    ohmic_spreading_number,
    reciprocal_surface,
    number_per_volume,
    thermal_kelvin,
    mapped_brick_members,
    arrival_owner_map,
    pedersen_sheet,
    electric_decay_rate,
):
    lists = mapped_brick_members[0, 0]
    owners = arrival_owner_map[0, 0]
    lat_rows, lon = electric_decay_rate.shape
    blocks = lon // LANES
    theta_rows = reciprocal_surface.shape[1]
    chunk_rows = CHUNK_FIELDS * blocks
    arguments = (
        induction_vector,
        reciprocal_surface,
        number_per_volume,
        thermal_kelvin,
        lists,
        owners,
        electric_decay_rate,
        ohmic_spreading_number,
    )
    sent, packet = pl.pallas_call(
        collect_kernel,
        out_shape=(shape_of(PEERS * chunk_rows, LANES), shape_of(4 * theta_rows, lon)),
        in_specs=[pl.BlockSpec(memory_space=pltpu.HBM)] * len(arguments),
        scratch_shapes=[pltpu.VMEM(a.shape, a.dtype) for a in arguments]
        + [pltpu.SemaphoreType.DMA((len(arguments),))],
        compiler_params=KERNEL_PARAMS,
        name="collect",
    )(*[pltpu.with_memory_space_constraint(a, pltpu.HBM) for a in arguments])
    arrived = exchange(sent.reshape(PEERS, chunk_rows, LANES), RING, SLOT_ORDER).reshape(PEERS * chunk_rows, LANES)
    other = lax.ppermute(packet, "pair", [(0, 1), (1, 0)])
    both = jnp.concatenate([packet, other], 0)
    even = lax.ppermute(both, RING, [(i, i ^ 1) for i in range(PEERS)])
    arrived, both, even = lax.optimization_barrier((arrived, both, even))
    odd_pairs = [(i, i + 1) for i in range(1, PEERS - 1, 2)]
    odd = lax.ppermute(both, RING, odd_pairs + [(j, i) for i, j in odd_pairs])
    copies = 2 * PEERS
    sum_rows = 2 * lat_rows * blocks
    sums = pl.pallas_call(
        deposit_kernel,
        out_shape=shape_of(copies * sum_rows, LANES),
        compiler_params=KERNEL_PARAMS,
        name="deposit",
    )(arrived, owners, pedersen_sheet)
    gathered = exchange(
        sums.reshape(copies, sum_rows, LANES), GROUP, [2 * d + p for d in SUM_ORDER for p in SUM_PAIRS]
    ).reshape(copies * sum_rows, LANES)
    advanced, boundary, potential = pl.pallas_call(
        finish_kernel,
        out_shape=(
            shape_of(3, 1, theta_rows, lon),
            shape_of(2, 1, theta_rows, lon),
            shape_of(lat_rows, lon),
        ),
        scratch_shapes=[pltpu.VMEM((8, 4 * theta_rows, lon), jnp.float32)],
        compiler_params=KERNEL_PARAMS,
        name="finish",
    )(gathered, arrived, lists, packet, other, even, odd)
    return advanced, boundary, potential


def local(*arguments):
    lists, decay, surface = arguments[5], arguments[8], arguments[2]
    fits = (
        lists.shape[2:] == (PEERS, decay.shape[1])
        and decay.shape == (2, 4 * LANES)
        and surface.shape == (1, 4, 4 * LANES)
        and lax.axis_size("pair") == 2
    )
    return short_plan(*arguments) if fits else stepwise(*arguments)


def solution(mesh):
    in_specs = (
        P(None, ("run", "pair"), ("tile", "sub"), None),
        P(("run", "pair"), ("tile", "sub"), None),
        P(("run", "pair"), ("tile", "sub"), None),
        P(("run", "pair"), ("tile", "sub"), None),
        P(("run", "pair"), ("tile", "sub"), None),
        P(("run", "pair"), ("tile", "sub"), None, None),
        P(("run", "pair"), ("tile", "sub"), None, None),
        P(("run", "pair"), ("tile", "sub"), None),
        P(("run", "tile", "sub"), None),
    )
    out_specs = (
        P(None, ("run", "pair"), ("tile", "sub"), None),
        P(None, ("run", "pair"), ("tile", "sub"), None),
        P(("run", "tile", "sub"), None),
    )
    return jax.shard_map(local, mesh=mesh, in_specs=in_specs, out_specs=out_specs, check_vma=False)
```

```python
import functools

import jax
import jax.numpy as jnp
from jax import lax
from jax.experimental import pallas as pl
from jax.experimental.pallas import tpu as pltpu
from jax.sharding import PartitionSpec as P

DIFF_STEPS = 4
SWEEPS = 8


def extended(cells, sides, width):
    for axis, dim in sides:
        count = lax.axis_size(axis)
        ends = count - 1
        head = lax.slice_in_dim(cells, 0, width, axis=dim)
        tail = lax.slice_in_dim(cells, cells.shape[dim] - width, cells.shape[dim], axis=dim)
        cells = jnp.concatenate(
            [
                lax.ppermute(tail, axis, [(i, (i + 1) % count) for i in range(ends)]),
                cells,
                lax.ppermute(head, axis, [((i + 1) % count, i) for i in range(ends)]),
            ],
            axis=dim,
        )
    return cells


def extend_cells(current_state):
    return extended(current_state, ((("tile", "sub"), 2), ("pair", 1)), 1)


def extend_columns(grid_values):
    return extended(grid_values, ((("tile", "sub"), 0),), 1)


def advance_field(current_state, padded, ohmic_spreading_number):
    neighbours = (
        padded[:, 2:, 1:-1] + padded[:, :-2, 1:-1] + padded[:, 1:-1, 2:] + padded[:, 1:-1, :-2]
    )
    neighbours = neighbours + jnp.roll(current_state, -1, 3) + jnp.roll(current_state, 1, 3)
    return current_state + ohmic_spreading_number * (neighbours - 6.0 * current_state)


def stepwise(
    induction_vector,
    ohmic_spreading_number,
    reciprocal_surface,
    number_per_volume,
    thermal_kelvin,
    mapped_brick_members,
    arrival_owner_map,
    pedersen_sheet,
    electric_decay_rate,
):
    padded = extend_cells(induction_vector)
    theta_diff = padded[2, 1:-1, 2:] - padded[2, 1:-1, :-2]
    phi_diff = jnp.roll(induction_vector[1], -1, 2) - jnp.roll(induction_vector[1], 1, 2)
    current = 0.5 * reciprocal_surface * (theta_diff - phi_diff)
    precipitation_power = 0.25 * number_per_volume * jnp.sqrt(thermal_kelvin)
    cell_lists = mapped_brick_members[0, 0]
    is_listed = cell_lists >= 0
    safe_index = jnp.where(is_listed, cell_lists, 0)
    sources = jnp.stack([current.reshape(-1), precipitation_power.reshape(-1)])
    payload = jnp.where(is_listed[None], sources[:, safe_index], 0.0)
    arrived = lax.all_to_all(payload, ("tile", "sub"), split_axis=1, concat_axis=1, tiled=True)
    land_columns = arrival_owner_map[0, 0]
    lat_rows, lon_cells = electric_decay_rate.shape
    column_count = lat_rows * lon_cells
    column_terms = (
        jnp.zeros((2, column_count), jnp.float32)
        .at[:, land_columns.reshape(-1)]
        .add(arrived.reshape(2, -1))
    )
    local_conductance = jnp.sum(pedersen_sheet, axis=0) + column_terms[1].reshape(
        lat_rows, lon_cells
    )
    aligned_current, conductance = lax.psum(
        (column_terms[0].reshape(lat_rows, lon_cells), local_conductance), "pair"
    )
    advanced = advance_field(induction_vector, padded, ohmic_spreading_number)
    for step_index in range(1, DIFF_STEPS):
        advanced = advance_field(advanced, extend_cells(advanced), ohmic_spreading_number)
    cond_rim = extend_columns(conductance)
    north_face = 0.5 * (conductance + cond_rim[:-2])
    south_face = 0.5 * (conductance + cond_rim[2:])
    east_face = 0.5 * (conductance + jnp.roll(conductance, -1, 1))
    west_face = 0.5 * (conductance + jnp.roll(conductance, 1, 1))
    diagonal = electric_decay_rate + north_face + south_face + east_face + west_face
    potential = aligned_current / diagonal
    for sweep_index in range(SWEEPS - 1):
        potential_rim = extend_columns(potential)
        potential = (
            aligned_current
            + north_face * potential_rim[:-2]
            + south_face * potential_rim[2:]
            + east_face * jnp.roll(potential, -1, 1)
            + west_face * jnp.roll(potential, 1, 1)
        ) / diagonal
    column_values = jnp.stack([potential, conductance]).reshape(2, -1)
    returned = lax.all_to_all(
        column_values[:, land_columns], ("tile", "sub"), split_axis=1, concat_axis=1, tiled=True
    )
    cell_count = current.size
    target = jnp.where(is_listed, cell_lists, cell_count)
    boundary = jnp.zeros((2, cell_count), jnp.float32).at[:, target].add(returned, mode="drop")
    boundary = boundary.reshape((2,) + current.shape)
    return (advanced, boundary, potential)


LANES = 128
PEERS = 8
RING = ("tile", "sub")
GROUP = ("tile", "sub", "pair")
CURRENT, FLUX, RIM_WEIGHT, CELL, OWNER, FIRST_ROW, LAST_ROW, DECAY = range(8)
CHUNK_FIELDS = 8
KERNEL_PARAMS = pltpu.CompilerParams(vmem_limit_bytes=4 * 2**20)


SLOT_ORDER = [5, 4, 3, 2, 1, 0, 7, 6]
SUM_ORDER = [5, 4, 3, 2, 1, 0, 7, 6]
SUM_PAIRS = (1, 0)


def by_position(values, width=LANES):
    row = lax.broadcasted_iota(jnp.int32, (PEERS, width), 0)
    out = jnp.zeros((PEERS, width), jnp.int32)
    for k, value in enumerate(values):
        out = jnp.where(row == k, value, out)
    return out


def take_rows(values, index):
    return jnp.take_along_axis(values, index, axis=0, mode="promise_in_bounds")


def neighbour_rows(values, order, step):
    wanted = [d + step for d in order]
    inside = [0 <= d < PEERS for d in wanted]
    index = by_position([order.index(d) if ok else 0 for d, ok in zip(wanted, inside)])
    valid = by_position([int(ok) for ok in inside]) == 1
    columns = blocks_of(values.shape[1] // LANES)
    return jnp.concatenate(
        [jnp.where(valid, take_rows(values[:, c], index), 0.0) for c in columns], 1
    )


def pick_lanes(row, lane):
    return jnp.take_along_axis(
        jnp.broadcast_to(row, lane.shape), lane, axis=1, mode="promise_in_bounds"
    )


def blocks_of(count):
    return [slice(b * LANES, (b + 1) * LANES) for b in range(count)]


def field_rows(field, block, blocks):
    return pl.ds(field * blocks + block, PEERS, stride=CHUNK_FIELDS * blocks)


def three_terms(values):
    first = values.astype(jnp.bfloat16)
    rest = values - first.astype(jnp.float32)
    second = rest.astype(jnp.bfloat16)
    third = (rest - second.astype(jnp.float32)).astype(jnp.bfloat16)
    return first, second, third


def one_hot_sums(rows, lanes, terms, row_count):
    total = None
    slots = rows.shape[1]
    row_at = lax.broadcasted_iota(jnp.int32, (row_count, slots), 0)
    lane_at = lax.broadcasted_iota(jnp.int32, (LANES, slots), 0)
    for s in range(rows.shape[0]):
        here = row_at == rows[s : s + 1]
        left = jnp.concatenate(
            [
                jnp.where(here, jnp.broadcast_to(t[s : s + 1], here.shape), 0.0)
                for t in terms
            ],
            axis=0,
        ).astype(jnp.bfloat16)
        right = jnp.where(lane_at == lanes[s : s + 1], 1.0, 0.0).astype(jnp.bfloat16)
        part = lax.dot_general(
            left, right, (((1,), (1,)), ((), ())), preferred_element_type=jnp.float32
        )
        total = part if total is None else total + part
    return total


def collect_kernel(*refs):
    count = 8
    here, (sent, packet), mine, (built, arrival, departure) = (
        refs[:count],
        refs[count : count + 2],
        refs[count + 2 : 2 * count + 2],
        refs[2 * count + 2 :],
    )
    copies = [pltpu.make_async_copy(here[k], mine[k], arrival.at[k]) for k in range(count)]
    for copy in copies:
        copy.start()
    for copy in copies:
        copy.wait()
    field, reciprocal, number, kelvin, lists, owners, decay, spreading = mine
    theta_rows, lon = reciprocal.shape[1:]
    blocks = lon // LANES
    spans = blocks_of(blocks)
    toward_theta = field[2, 0]
    toward_phi = field[1, 0]
    order = by_position(SLOT_ORDER)
    own_decay = jnp.where(lax.axis_index("pair") == 0, decay[0:1], decay[1:2])
    for b, span in enumerate(spans):
        built[:, OWNER * blocks + b, :] = take_rows(owners[:, span], order).astype(jnp.float32)
        for k, row in (
            (FIRST_ROW, toward_theta[:1]),
            (LAST_ROW, toward_theta[-1:]),
            (DECAY, own_decay),
        ):
            built[:, k * blocks + b, :] = jnp.broadcast_to(row[:, span], (PEERS, LANES))
    parts = [slice(OWNER * blocks, CHUNK_FIELDS * blocks), slice(0, OWNER * blocks)]
    leaving = [
        pltpu.make_async_copy(built.at[:, part, :], sent.at[:, part, :], departure.at[k])
        for k, part in enumerate(parts)
    ]
    leaving[0].start()
    zero_row = jnp.zeros((1, lon), jnp.float32)
    half = 0.5 * reciprocal[0]
    theta_diff = jnp.concatenate([toward_theta[1:], zero_row], 0) - jnp.concatenate(
        [zero_row, toward_theta[:-1]], 0
    )
    phi_diff = pltpu.roll(toward_phi, lon - 1, 1) - pltpu.roll(toward_phi, 1, 1)
    current = half * (theta_diff - phi_diff)
    flux = 0.25 * number[0] * jnp.sqrt(kelvin[0])
    for b, span in enumerate(spans):
        cell = take_rows(lists[:, span], order)
        lane = cell & (LANES - 1)
        row = cell >> 7
        taken = [jnp.zeros(cell.shape, jnp.float32)] * 3
        for theta in range(theta_rows):
            for c, source in enumerate(spans):
                here = row == theta * blocks + c
                at = slice(theta, theta + 1)
                tables = [current[at, source], flux[at, source]]
                if theta == 0:
                    tables.append(-half[at, source])
                if theta == theta_rows - 1:
                    tables.append(half[at, source])
                for k, table in enumerate(tables):
                    taken[k] = jnp.where(here, pick_lanes(table, lane), taken[k])
        for k, value in enumerate(taken + [cell.astype(jnp.float32)]):
            built[:, k * blocks + b, :] = value
    leaving[1].start()
    for b, span in enumerate(spans):
        for k in range(4):
            at = (b * 4 + k) * theta_rows
            packet[at : at + theta_rows] = (field[k, 0] if k < 3 else spreading[0])[:, span]
    for copy in leaving:
        copy.wait()


def prepare_kernel(owners, sheet, columns, levels, mine, sheets, arrival):
    copies = [
        pltpu.make_async_copy(owners, mine, arrival.at[0]),
        pltpu.make_async_copy(sheet, sheets, arrival.at[1]),
    ]
    for copy in copies:
        copy.start()
    for copy in copies:
        copy.wait()
    order = by_position(SLOT_ORDER)
    spans = blocks_of(columns.shape[1] // LANES)
    level_sum = jnp.sum(sheets[...], axis=0)
    for b, span in enumerate(spans):
        columns[:, span] = take_rows(mine[:, span], order)
        for i in range(level_sum.shape[0]):
            levels[i * len(spans) + b : i * len(spans) + b + 1] = level_sum[i : i + 1, span]


def deposit_kernel(arrived, columns, levels, sums):
    lon = columns.shape[1]
    blocks = lon // LANES
    rows = levels.shape[0]
    above = [
        neighbour_rows(arrived[field_rows(LAST_ROW, b, blocks), :], SLOT_ORDER, -1) for b in range(blocks)
    ]
    below = [
        neighbour_rows(arrived[field_rows(FIRST_ROW, b, blocks), :], SLOT_ORDER, 1) for b in range(blocks)
    ]
    currents, fluxes = [], []
    for b in range(blocks):
        cell = arrived[field_rows(CELL, b, blocks), :].astype(jnp.int32)
        phi_block = (cell >> 7) & (blocks - 1)
        lane = cell & (LANES - 1)
        rim = jnp.zeros((PEERS, LANES), jnp.float32)
        for c in range(blocks):
            found = jnp.where(
                cell < lon, pick_lanes(above[c], lane), pick_lanes(below[c], lane)
            )
            rim = jnp.where(phi_block == c, found, rim)
        weight = arrived[field_rows(RIM_WEIGHT, b, blocks), :]
        currents.append(arrived[field_rows(CURRENT, b, blocks), :] + weight * rim)
        fluxes.append(arrived[field_rows(FLUX, b, blocks), :])
    column = columns[...]
    terms = three_terms(jnp.concatenate(currents, 1)) + three_terms(jnp.concatenate(fluxes, 1))
    total = one_hot_sums(
        column >> 7, column & (LANES - 1), [t.astype(jnp.float32) for t in terms], rows
    )
    parts = [total[k * rows : (k + 1) * rows] for k in range(6)]
    current = parts[0] + parts[1] + parts[2]
    flux = parts[3] + parts[4] + parts[5]
    both = jnp.concatenate([current, flux + levels[...]], 0)
    for k in range(sums.shape[0]):
        sums[k] = both


def footpoint_kernel(arrived, lists, found, *, lat_rows):
    lon = lists.shape[1]
    blocks = lon // LANES
    owner = jnp.concatenate(
        [arrived[field_rows(OWNER, b, blocks), :] for b in range(blocks)], 1
    ).astype(jnp.int32)
    device = by_position(SLOT_ORDER, lon)
    row = (owner >> 7) + device * (lat_rows * blocks) + 1
    lane = owner & (LANES - 1)
    order = by_position(SLOT_ORDER)
    cell = jnp.concatenate([take_rows(lists[:, span], order) for span in blocks_of(blocks)], 1)
    found[...] = one_hot_sums(
        cell >> 7,
        cell & (LANES - 1),
        [row.astype(jnp.float32), lane.astype(jnp.float32)],
        found.shape[0] // 2,
    ).astype(jnp.int32)


def advance_body(own, other, odd, advanced, planes):
    theta_rows = advanced.shape[2]
    spans = blocks_of(advanced.shape[3] // LANES)
    span_rows = len(spans) * 4 * theta_rows
    top, here = 2 * theta_rows, slice(2 * theta_rows, 6 * theta_rows)
    is_odd = (lax.axis_index(RING) & 1) == 1
    margin = jnp.zeros((2 * theta_rows, LANES), jnp.float32)
    for shell, bricks in enumerate((own, other)):
        for k in range(4):
            for b in range(len(spans)):
                at = (shell, k, b)
                start = (b * 4 + k) * theta_rows
                middle = bricks[start : start + theta_rows]
                by_even = bricks[span_rows + start : span_rows + start + theta_rows]
                by_odd = odd[shell * span_rows + start : shell * span_rows + start + theta_rows]
                for buffer in range(2):
                    planes[buffer, *at, :top] = margin
                    planes[buffer, *at, 6 * theta_rows :] = margin
                planes[0, *at, 4 * theta_rows : 6 * theta_rows] = margin
                planes[0, *at, top : top + theta_rows] = jnp.where(is_odd, by_even, by_odd)
                planes[0, *at, top + theta_rows : top + 2 * theta_rows] = middle
                planes[0, *at, top + 2 * theta_rows : top + 3 * theta_rows] = jnp.where(
                    is_odd, by_odd, by_even
                )
    lane = lax.broadcasted_iota(jnp.int32, (4 * theta_rows, LANES), 1)
    first, last = lane == 0, lane == LANES - 1
    for step in range(DIFF_STEPS):
        now, later = step % 2, 1 - step % 2
        for k in range(3):
            for shell in range(2):
                if step == DIFF_STEPS - 1 and shell == 1:
                    continue
                state = [planes[now, shell, k, b, here] for b in range(len(spans))]
                ahead = [pltpu.roll(x, LANES - 1, 1) for x in state]
                behind = [pltpu.roll(x, 1, 1) for x in state]
                for b, span in enumerate(spans):
                    at = (now, shell, k, b)
                    around = planes[now, 1 - shell, k, b, here] + planes[
                        *at, top + 1 : 6 * theta_rows + 1
                    ]
                    around = around + planes[*at, top - 1 : 6 * theta_rows - 1]
                    around = around + jnp.where(last, ahead[(b + 1) % len(spans)], ahead[b])
                    around = around + jnp.where(first, behind[b - 1], behind[b])
                    spreading = planes[0, shell, 3, b, here]
                    result = state[b] + spreading * (around - 6.0 * state[b])
                    if step == DIFF_STEPS - 1:
                        advanced[k, 0, :, span] = result[theta_rows : 2 * theta_rows]
                    else:
                        planes[later, shell, k, b, here] = result


def solve_body(sums, arrived, other, found, boundary, potential, tables):
    lon = potential.shape[1]
    blocks = lon // LANES
    rows = 2 * blocks
    cell_rows = boundary.shape[2] * blocks
    row, lane = found[:cell_rows], found[cell_rows:]
    ring = by_position(SUM_ORDER, lon)
    place_of = by_position([SLOT_ORDER.index(d) for d in SUM_ORDER])

    def summed(term, lat):
        return jnp.concatenate(
            [
                sum(
                    sums[pl.ds((pair * 2 + term) * rows + lat * blocks + b, PEERS, stride=4 * rows), :]
                    for pair in range(2)
                )
                for b in range(blocks)
            ],
            1,
        )

    start = other.shape[0] - PEERS * blocks
    mine = [arrived[field_rows(DECAY, b, blocks), :] for b in range(blocks)]
    theirs = [other[pl.ds(start + b, PEERS, stride=blocks), :] for b in range(blocks)]
    mine, theirs = (
        jnp.concatenate([take_rows(part, place_of) for part in parts], 1)
        for parts in (mine, theirs)
    )
    first = lax.axis_index("pair") == 0
    decay_rows = [jnp.where(first, mine, theirs), jnp.where(first, theirs, mine)]

    def before(values):
        return neighbour_rows(values, SUM_ORDER, -1)

    def after(values):
        return neighbour_rows(values, SUM_ORDER, 1)

    def east(values):
        return pltpu.roll(values, lon - 1, 1)

    def west(values):
        return pltpu.roll(values, 1, 1)

    aligned = [summed(0, 0), summed(0, 1)]
    conductance = [summed(1, 0), summed(1, 1)]
    faces = []
    middle = 0.5 * (conductance[0] + conductance[1])
    north = (0.5 * (conductance[0] + before(conductance[1])), middle)
    south = (middle, 0.5 * (conductance[1] + after(conductance[0])))
    level = []
    for lat in range(2):
        here = conductance[lat]
        east_face = 0.5 * (here + east(here))
        west_face = 0.5 * (here + west(here))
        diagonal = decay_rows[lat] + north[lat] + south[lat] + east_face + west_face
        inverse = 1.0 / diagonal
        faces.append([f * inverse for f in (north[lat], south[lat], east_face, west_face)])
        aligned[lat] = aligned[lat] * inverse
        level.append(aligned[lat])
    for _ in range(SWEEPS - 1):
        around = ((before(level[1]), level[1]), (level[0], after(level[0])))
        level = [
            (aligned[lat] + faces[lat][0] * around[lat][0] + faces[lat][1] * around[lat][1])
            + (faces[lat][2] * east(level[lat]) + faces[lat][3] * west(level[lat]))
            for lat in range(2)
        ]
    me = lax.axis_index(RING)
    for lat in range(2):
        potential[lat : lat + 1] = jnp.sum(
            jnp.where(ring == me, level[lat], 0.0), axis=0, keepdims=True
        )
    for lat in range(2):
        for b, span in enumerate(blocks_of(blocks)):
            at = pl.ds(lat * blocks + b, PEERS, stride=rows)
            tables[0, at, :] = level[lat][:, span]
            tables[1, at, :] = conductance[lat][:, span]
    for half in range(cell_rows // PEERS):
        part = slice(half * PEERS, (half + 1) * PEERS)
        for k in range(2):
            taken = jnp.zeros((PEERS, LANES), jnp.float32)
            for place, device in enumerate(SUM_ORDER):
                for r in range(rows):
                    at = place * rows + r
                    one = pick_lanes(tables[k, at : at + 1, :], lane[part])
                    taken = jnp.where(row[part] == device * rows + r + 1, one, taken)
            for r in range(PEERS):
                theta, b = divmod(half * PEERS + r, blocks)
                boundary[k, 0, theta : theta + 1, blocks_of(blocks)[b]] = taken[r : r + 1]


def finish_kernel(
    sums, arrived, found, own, other, odd, advanced, boundary, potential, planes, tables
):
    advance_body(own, other, odd, advanced, planes)
    solve_body(sums, arrived, other, found, boundary, potential, tables)


def shape_of(*dims):
    return jax.ShapeDtypeStruct(dims, jnp.float32)


def exchange(chunks, axes, order):
    return lax.all_to_all(
        chunks, axes, split_axis=0, concat_axis=0, axis_index_groups=[order], tiled=True
    )


def short_plan(
    induction_vector,
    ohmic_spreading_number,
    reciprocal_surface,
    number_per_volume,
    thermal_kelvin,
    mapped_brick_members,
    arrival_owner_map,
    pedersen_sheet,
    electric_decay_rate,
):
    lists = mapped_brick_members[0, 0]
    owners = arrival_owner_map[0, 0]
    lat_rows, lon = electric_decay_rate.shape
    blocks = lon // LANES
    theta_rows = reciprocal_surface.shape[1]
    chunk_rows = CHUNK_FIELDS * blocks
    arguments = (
        induction_vector,
        reciprocal_surface,
        number_per_volume,
        thermal_kelvin,
        lists,
        owners,
        electric_decay_rate,
        ohmic_spreading_number,
    )
    sent, packet = pl.pallas_call(
        collect_kernel,
        out_shape=(
            shape_of(PEERS, chunk_rows, LANES),
            shape_of(4 * theta_rows * blocks, LANES),
        ),
        in_specs=[pl.BlockSpec(memory_space=pltpu.HBM)] * len(arguments),
        out_specs=(
            pl.BlockSpec(memory_space=pltpu.HBM),
            pl.BlockSpec(memory_space=pltpu.VMEM),
        ),
        scratch_shapes=[pltpu.VMEM(a.shape, a.dtype) for a in arguments]
        + [
            pltpu.VMEM((PEERS, chunk_rows, LANES), jnp.float32),
            pltpu.SemaphoreType.DMA((len(arguments),)),
            pltpu.SemaphoreType.DMA((2,)),
        ],
        compiler_params=KERNEL_PARAMS,
        name="collect",
    )(*[pltpu.with_memory_space_constraint(a, pltpu.HBM) for a in arguments])
    arrived = exchange(sent, RING, SLOT_ORDER).reshape(PEERS * chunk_rows, LANES)
    columns, levels = pl.pallas_call(
        prepare_kernel,
        out_shape=(
            jax.ShapeDtypeStruct((PEERS, lon), jnp.int32),
            shape_of(lat_rows * blocks, LANES),
        ),
        in_specs=[pl.BlockSpec(memory_space=pltpu.HBM)] * 2,
        scratch_shapes=[
            pltpu.VMEM(owners.shape, jnp.int32),
            pltpu.VMEM(pedersen_sheet.shape, jnp.float32),
            pltpu.SemaphoreType.DMA((2,)),
        ],
        compiler_params=KERNEL_PARAMS,
        name="prepare",
    )(*[pltpu.with_memory_space_constraint(a, pltpu.HBM) for a in (owners, pedersen_sheet)])
    even = lax.ppermute(packet, RING, [(i, i ^ 1) for i in range(PEERS)])
    arrived, even, columns, levels = lax.optimization_barrier((arrived, even, columns, levels))
    decays = arrived.reshape(PEERS, chunk_rows, LANES)[:, DECAY * blocks : (DECAY + 1) * blocks]
    own = jnp.concatenate([packet, even, decays.reshape(PEERS * blocks, LANES)], 0)
    other = lax.ppermute(own, "pair", [(0, 1), (1, 0)])
    copies = 2 * PEERS
    sum_rows = 2 * lat_rows * blocks
    sums = pl.pallas_call(
        deposit_kernel,
        out_shape=shape_of(copies, sum_rows, LANES),
        compiler_params=KERNEL_PARAMS,
        name="deposit",
    )(arrived, columns, levels)
    sums, other = lax.optimization_barrier((sums, other))
    both = jnp.concatenate([packet, other[: packet.shape[0]]], 0)
    odd_pairs = [(i, i + 1) for i in range(1, PEERS - 1, 2)]
    odd = lax.ppermute(both, RING, odd_pairs + [(j, i) for i, j in odd_pairs])
    gathered = exchange(
        sums, GROUP, [2 * d + p for d in SUM_ORDER for p in SUM_PAIRS]
    ).reshape(copies * sum_rows, LANES)
    found = pl.pallas_call(
        functools.partial(footpoint_kernel, lat_rows=lat_rows),
        out_shape=jax.ShapeDtypeStruct((2 * theta_rows * blocks, LANES), jnp.int32),
        compiler_params=KERNEL_PARAMS,
        name="footpoints",
    )(arrived, lists)
    advanced, boundary, potential = pl.pallas_call(
        finish_kernel,
        out_shape=(
            shape_of(3, 1, theta_rows, lon),
            shape_of(2, 1, theta_rows, lon),
            shape_of(lat_rows, lon),
        ),
        scratch_shapes=[
            pltpu.VMEM((2, 2, 4, blocks, 8 * theta_rows, LANES), jnp.float32),
            pltpu.VMEM((2, PEERS * lat_rows * blocks, LANES), jnp.float32),
        ],
        compiler_params=KERNEL_PARAMS,
        name="finish",
    )(gathered, arrived, found, own, other, odd)
    return advanced, boundary, potential


def local(*arguments):
    lists, decay, surface = arguments[5], arguments[8], arguments[2]
    fits = (
        lists.shape[2:] == (PEERS, decay.shape[1])
        and decay.shape == (2, 4 * LANES)
        and surface.shape == (1, 4, 4 * LANES)
        and lax.axis_size("pair") == 2
    )
    return short_plan(*arguments) if fits else stepwise(*arguments)


def solution(mesh):
    in_specs = (
        P(None, ("run", "pair"), ("tile", "sub"), None),
        P(("run", "pair"), ("tile", "sub"), None),
        P(("run", "pair"), ("tile", "sub"), None),
        P(("run", "pair"), ("tile", "sub"), None),
        P(("run", "pair"), ("tile", "sub"), None),
        P(("run", "pair"), ("tile", "sub"), None, None),
        P(("run", "pair"), ("tile", "sub"), None, None),
        P(("run", "pair"), ("tile", "sub"), None),
        P(("run", "tile", "sub"), None),
    )
    out_specs = (
        P(None, ("run", "pair"), ("tile", "sub"), None),
        P(None, ("run", "pair"), ("tile", "sub"), None),
        P(("run", "tile", "sub"), None),
    )
    return jax.shard_map(local, mesh=mesh, in_specs=in_specs, out_specs=out_specs, check_vma=False)
```

```python
import functools

import jax
import jax.numpy as jnp
from jax import lax
from jax.experimental import pallas as pl
from jax.experimental.pallas import tpu as pltpu
from jax.sharding import PartitionSpec as P

DIFF_STEPS = 4
SWEEPS = 8


def extended(cells, sides, width):
    for axis, dim in sides:
        count = lax.axis_size(axis)
        ends = count - 1
        head = lax.slice_in_dim(cells, 0, width, axis=dim)
        tail = lax.slice_in_dim(cells, cells.shape[dim] - width, cells.shape[dim], axis=dim)
        cells = jnp.concatenate(
            [
                lax.ppermute(tail, axis, [(i, (i + 1) % count) for i in range(ends)]),
                cells,
                lax.ppermute(head, axis, [((i + 1) % count, i) for i in range(ends)]),
            ],
            axis=dim,
        )
    return cells


def extend_cells(current_state):
    return extended(current_state, ((("tile", "sub"), 2), ("pair", 1)), 1)


def extend_columns(grid_values):
    return extended(grid_values, ((("tile", "sub"), 0),), 1)


def advance_field(current_state, padded, ohmic_spreading_number):
    neighbours = (
        padded[:, 2:, 1:-1] + padded[:, :-2, 1:-1] + padded[:, 1:-1, 2:] + padded[:, 1:-1, :-2]
    )
    neighbours = neighbours + jnp.roll(current_state, -1, 3) + jnp.roll(current_state, 1, 3)
    return current_state + ohmic_spreading_number * (neighbours - 6.0 * current_state)


def stepwise(
    induction_vector,
    ohmic_spreading_number,
    reciprocal_surface,
    number_per_volume,
    thermal_kelvin,
    mapped_brick_members,
    arrival_owner_map,
    pedersen_sheet,
    electric_decay_rate,
):
    padded = extend_cells(induction_vector)
    theta_diff = padded[2, 1:-1, 2:] - padded[2, 1:-1, :-2]
    phi_diff = jnp.roll(induction_vector[1], -1, 2) - jnp.roll(induction_vector[1], 1, 2)
    current = 0.5 * reciprocal_surface * (theta_diff - phi_diff)
    precipitation_power = 0.25 * number_per_volume * jnp.sqrt(thermal_kelvin)
    cell_lists = mapped_brick_members[0, 0]
    is_listed = cell_lists >= 0
    safe_index = jnp.where(is_listed, cell_lists, 0)
    sources = jnp.stack([current.reshape(-1), precipitation_power.reshape(-1)])
    payload = jnp.where(is_listed[None], sources[:, safe_index], 0.0)
    arrived = lax.all_to_all(payload, ("tile", "sub"), split_axis=1, concat_axis=1, tiled=True)
    land_columns = arrival_owner_map[0, 0]
    lat_rows, lon_cells = electric_decay_rate.shape
    column_count = lat_rows * lon_cells
    column_terms = (
        jnp.zeros((2, column_count), jnp.float32)
        .at[:, land_columns.reshape(-1)]
        .add(arrived.reshape(2, -1))
    )
    local_conductance = jnp.sum(pedersen_sheet, axis=0) + column_terms[1].reshape(
        lat_rows, lon_cells
    )
    aligned_current, conductance = lax.psum(
        (column_terms[0].reshape(lat_rows, lon_cells), local_conductance), "pair"
    )
    advanced = advance_field(induction_vector, padded, ohmic_spreading_number)
    for step_index in range(1, DIFF_STEPS):
        advanced = advance_field(advanced, extend_cells(advanced), ohmic_spreading_number)
    cond_rim = extend_columns(conductance)
    north_face = 0.5 * (conductance + cond_rim[:-2])
    south_face = 0.5 * (conductance + cond_rim[2:])
    east_face = 0.5 * (conductance + jnp.roll(conductance, -1, 1))
    west_face = 0.5 * (conductance + jnp.roll(conductance, 1, 1))
    diagonal = electric_decay_rate + north_face + south_face + east_face + west_face
    potential = aligned_current / diagonal
    for sweep_index in range(SWEEPS - 1):
        potential_rim = extend_columns(potential)
        potential = (
            aligned_current
            + north_face * potential_rim[:-2]
            + south_face * potential_rim[2:]
            + east_face * jnp.roll(potential, -1, 1)
            + west_face * jnp.roll(potential, 1, 1)
        ) / diagonal
    column_values = jnp.stack([potential, conductance]).reshape(2, -1)
    returned = lax.all_to_all(
        column_values[:, land_columns], ("tile", "sub"), split_axis=1, concat_axis=1, tiled=True
    )
    cell_count = current.size
    target = jnp.where(is_listed, cell_lists, cell_count)
    boundary = jnp.zeros((2, cell_count), jnp.float32).at[:, target].add(returned, mode="drop")
    boundary = boundary.reshape((2,) + current.shape)
    return (advanced, boundary, potential)


LANES = 128
PEERS = 8
RING = ("tile", "sub")
GROUP = ("tile", "sub", "pair")
CURRENT, FLUX, RIM_WEIGHT, CELL, OWNER, FIRST_ROW, LAST_ROW, DECAY = range(8)
CHUNK_FIELDS = 8
KERNEL_PARAMS = pltpu.CompilerParams(vmem_limit_bytes=4 * 2**20)


SLOT_ORDER = [5, 4, 3, 2, 1, 0, 7, 6]
SUM_ORDER = [5, 4, 3, 2, 1, 0, 7, 6]
SUM_PAIRS = (1, 0)


def by_position(values, width=LANES):
    row = lax.broadcasted_iota(jnp.int32, (PEERS, width), 0)
    out = jnp.zeros((PEERS, width), jnp.int32)
    for k, value in enumerate(values):
        out = jnp.where(row == k, value, out)
    return out


def take_rows(values, index):
    return jnp.take_along_axis(values, index, axis=0, mode="promise_in_bounds")


def neighbour_rows(values, order, step):
    wanted = [d + step for d in order]
    inside = [0 <= d < PEERS for d in wanted]
    index = by_position([order.index(d) if ok else 0 for d, ok in zip(wanted, inside)])
    valid = by_position([int(ok) for ok in inside]) == 1
    columns = blocks_of(values.shape[1] // LANES)
    return jnp.concatenate(
        [jnp.where(valid, take_rows(values[:, c], index), 0.0) for c in columns], 1
    )


def pick_lanes(row, lane):
    return jnp.take_along_axis(
        jnp.broadcast_to(row, lane.shape), lane, axis=1, mode="promise_in_bounds"
    )


def blocks_of(count):
    return [slice(b * LANES, (b + 1) * LANES) for b in range(count)]


def field_rows(field, block, blocks):
    return pl.ds(field * blocks + block, PEERS, stride=CHUNK_FIELDS * blocks)


def three_terms(values):
    first = values.astype(jnp.bfloat16)
    rest = values - first.astype(jnp.float32)
    second = rest.astype(jnp.bfloat16)
    third = (rest - second.astype(jnp.float32)).astype(jnp.bfloat16)
    return first, second, third


def one_hot_sums(rows, lanes, terms, row_count):
    total = None
    slots = rows.shape[1]
    row_at = lax.broadcasted_iota(jnp.int32, (row_count, slots), 0)
    lane_at = lax.broadcasted_iota(jnp.int32, (LANES, slots), 0)
    for s in range(rows.shape[0]):
        here = row_at == rows[s : s + 1]
        left = jnp.concatenate(
            [
                jnp.where(here, jnp.broadcast_to(t[s : s + 1], here.shape), 0.0)
                for t in terms
            ],
            axis=0,
        ).astype(jnp.bfloat16)
        right = jnp.where(lane_at == lanes[s : s + 1], 1.0, 0.0).astype(jnp.bfloat16)
        part = lax.dot_general(
            left, right, (((1,), (1,)), ((), ())), preferred_element_type=jnp.float32
        )
        total = part if total is None else total + part
    return total


def collect_kernel(*refs):
    count = 8
    here, (sent, packet), mine, (built, arrival, departure) = (
        refs[:count],
        refs[count : count + 2],
        refs[count + 2 : 2 * count + 2],
        refs[2 * count + 2 :],
    )
    copies = [pltpu.make_async_copy(here[k], mine[k], arrival.at[k]) for k in range(count)]
    for copy in copies:
        copy.start()
    for copy in copies:
        copy.wait()
    field, reciprocal, number, kelvin, lists, owners, decay, spreading = mine
    theta_rows, lon = reciprocal.shape[1:]
    blocks = lon // LANES
    spans = blocks_of(blocks)
    toward_theta = field[2, 0]
    toward_phi = field[1, 0]
    order = by_position(SLOT_ORDER)
    own_decay = jnp.where(lax.axis_index("pair") == 0, decay[0:1], decay[1:2])
    for b, span in enumerate(spans):
        built[:, OWNER * blocks + b, :] = take_rows(owners[:, span], order).astype(jnp.float32)
        for k, row in (
            (FIRST_ROW, toward_theta[:1]),
            (LAST_ROW, toward_theta[-1:]),
            (DECAY, own_decay),
        ):
            built[:, k * blocks + b, :] = jnp.broadcast_to(row[:, span], (PEERS, LANES))
    parts = [slice(OWNER * blocks, CHUNK_FIELDS * blocks), slice(0, OWNER * blocks)]
    leaving = [
        pltpu.make_async_copy(built.at[:, part, :], sent.at[:, part, :], departure.at[k])
        for k, part in enumerate(parts)
    ]
    leaving[0].start()
    zero_row = jnp.zeros((1, lon), jnp.float32)
    half = 0.5 * reciprocal[0]
    theta_diff = jnp.concatenate([toward_theta[1:], zero_row], 0) - jnp.concatenate(
        [zero_row, toward_theta[:-1]], 0
    )
    phi_diff = pltpu.roll(toward_phi, lon - 1, 1) - pltpu.roll(toward_phi, 1, 1)
    current = half * (theta_diff - phi_diff)
    flux = 0.25 * number[0] * jnp.sqrt(kelvin[0])
    for b, span in enumerate(spans):
        cell = take_rows(lists[:, span], order)
        lane = cell & (LANES - 1)
        row = cell >> 7
        taken = [jnp.zeros(cell.shape, jnp.float32)] * 3
        for theta in range(theta_rows):
            for c, source in enumerate(spans):
                here = row == theta * blocks + c
                at = slice(theta, theta + 1)
                tables = [current[at, source], flux[at, source]]
                if theta == 0:
                    tables.append(-half[at, source])
                if theta == theta_rows - 1:
                    tables.append(half[at, source])
                for k, table in enumerate(tables):
                    taken[k] = jnp.where(here, pick_lanes(table, lane), taken[k])
        for k, value in enumerate(taken + [cell.astype(jnp.float32)]):
            built[:, k * blocks + b, :] = value
    leaving[1].start()
    for b, span in enumerate(spans):
        for k in range(4):
            at = (b * 4 + k) * theta_rows
            packet[at : at + theta_rows] = (field[k, 0] if k < 3 else spreading[0])[:, span]
    for copy in leaving:
        copy.wait()


def prepare_kernel(owners, sheet, columns, levels, mine, sheets, arrival):
    copies = [
        pltpu.make_async_copy(owners, mine, arrival.at[0]),
        pltpu.make_async_copy(sheet, sheets, arrival.at[1]),
    ]
    for copy in copies:
        copy.start()
    for copy in copies:
        copy.wait()
    order = by_position(SLOT_ORDER)
    spans = blocks_of(columns.shape[1] // LANES)
    level_sum = jnp.sum(sheets[...], axis=0)
    for b, span in enumerate(spans):
        columns[:, span] = take_rows(mine[:, span], order)
        for i in range(level_sum.shape[0]):
            levels[i * len(spans) + b : i * len(spans) + b + 1] = level_sum[i : i + 1, span]


def deposit_kernel(arrived, columns, levels, sums):
    lon = columns.shape[1]
    blocks = lon // LANES
    rows = levels.shape[0]
    above = [
        neighbour_rows(arrived[field_rows(LAST_ROW, b, blocks), :], SLOT_ORDER, -1) for b in range(blocks)
    ]
    below = [
        neighbour_rows(arrived[field_rows(FIRST_ROW, b, blocks), :], SLOT_ORDER, 1) for b in range(blocks)
    ]
    currents, fluxes = [], []
    for b in range(blocks):
        cell = arrived[field_rows(CELL, b, blocks), :].astype(jnp.int32)
        phi_block = (cell >> 7) & (blocks - 1)
        lane = cell & (LANES - 1)
        rim = jnp.zeros((PEERS, LANES), jnp.float32)
        for c in range(blocks):
            found = jnp.where(
                cell < lon, pick_lanes(above[c], lane), pick_lanes(below[c], lane)
            )
            rim = jnp.where(phi_block == c, found, rim)
        weight = arrived[field_rows(RIM_WEIGHT, b, blocks), :]
        currents.append(arrived[field_rows(CURRENT, b, blocks), :] + weight * rim)
        fluxes.append(arrived[field_rows(FLUX, b, blocks), :])
    column = columns[...]
    terms = three_terms(jnp.concatenate(currents, 1)) + three_terms(jnp.concatenate(fluxes, 1))
    total = one_hot_sums(
        column >> 7, column & (LANES - 1), [t.astype(jnp.float32) for t in terms], rows
    )
    parts = [total[k * rows : (k + 1) * rows] for k in range(6)]
    current = parts[0] + parts[1] + parts[2]
    flux = parts[3] + parts[4] + parts[5]
    both = jnp.concatenate([current, flux + levels[...]], 0)
    for k in range(sums.shape[0]):
        sums[k] = both


def footpoint_kernel(arrived, lists, found, *, lat_rows):
    lon = lists.shape[1]
    blocks = lon // LANES
    owner = jnp.concatenate(
        [arrived[field_rows(OWNER, b, blocks), :] for b in range(blocks)], 1
    ).astype(jnp.int32)
    device = by_position(SLOT_ORDER, lon)
    row = (owner >> 7) + device * (lat_rows * blocks) + 1
    lane = owner & (LANES - 1)
    order = by_position(SLOT_ORDER)
    cell = jnp.concatenate([take_rows(lists[:, span], order) for span in blocks_of(blocks)], 1)
    found[...] = one_hot_sums(
        cell >> 7,
        cell & (LANES - 1),
        [row.astype(jnp.float32), lane.astype(jnp.float32)],
        found.shape[0] // 2,
    ).astype(jnp.int32)


def advance_kernel(own, other, advanced, planes):
    theta_rows = advanced.shape[2]
    spans = blocks_of(advanced.shape[3] // LANES)
    span_rows = len(spans) * 4 * theta_rows
    top, here = 2 * theta_rows, slice(2 * theta_rows, 6 * theta_rows)
    is_odd = (lax.axis_index(RING) & 1) == 1
    margin = jnp.zeros((2 * theta_rows, LANES), jnp.float32)
    for shell, bricks in enumerate((own, other)):
        for k in range(4):
            for b in range(len(spans)):
                at = (shell, k, b)
                start = (b * 4 + k) * theta_rows
                middle = bricks[start : start + theta_rows]
                by_even = bricks[span_rows + start : span_rows + start + theta_rows]
                by_odd = bricks[2 * span_rows + start : 2 * span_rows + start + theta_rows]
                for buffer in range(2):
                    planes[buffer, *at, :top] = margin
                    planes[buffer, *at, 6 * theta_rows :] = margin
                planes[0, *at, 4 * theta_rows : 6 * theta_rows] = margin
                planes[0, *at, top : top + theta_rows] = jnp.where(is_odd, by_even, by_odd)
                planes[0, *at, top + theta_rows : top + 2 * theta_rows] = middle
                planes[0, *at, top + 2 * theta_rows : top + 3 * theta_rows] = jnp.where(
                    is_odd, by_odd, by_even
                )
    lane = lax.broadcasted_iota(jnp.int32, (4 * theta_rows, LANES), 1)
    first, last = lane == 0, lane == LANES - 1
    for step in range(DIFF_STEPS):
        now, later = step % 2, 1 - step % 2
        for k in range(3):
            for shell in range(2):
                if step == DIFF_STEPS - 1 and shell == 1:
                    continue
                state = [planes[now, shell, k, b, here] for b in range(len(spans))]
                ahead = [pltpu.roll(x, LANES - 1, 1) for x in state]
                behind = [pltpu.roll(x, 1, 1) for x in state]
                for b, span in enumerate(spans):
                    at = (now, shell, k, b)
                    around = planes[now, 1 - shell, k, b, here] + planes[
                        *at, top + 1 : 6 * theta_rows + 1
                    ]
                    around = around + planes[*at, top - 1 : 6 * theta_rows - 1]
                    around = around + jnp.where(last, ahead[(b + 1) % len(spans)], ahead[b])
                    around = around + jnp.where(first, behind[b - 1], behind[b])
                    spreading = planes[0, shell, 3, b, here]
                    result = state[b] + spreading * (around - 6.0 * state[b])
                    if step == DIFF_STEPS - 1:
                        advanced[k, 0, :, span] = result[theta_rows : 2 * theta_rows]
                    else:
                        planes[later, shell, k, b, here] = result


def solve_kernel(sums, arrived, other, found, boundary, potential, tables):
    lon = potential.shape[1]
    blocks = lon // LANES
    rows = 2 * blocks
    cell_rows = boundary.shape[2] * blocks
    row, lane = found[:cell_rows], found[cell_rows:]
    ring = by_position(SUM_ORDER, lon)
    place_of = by_position([SLOT_ORDER.index(d) for d in SUM_ORDER])

    def summed(term, lat):
        return jnp.concatenate(
            [
                sum(
                    sums[pl.ds((pair * 2 + term) * rows + lat * blocks + b, PEERS, stride=4 * rows), :]
                    for pair in range(2)
                )
                for b in range(blocks)
            ],
            1,
        )

    start = other.shape[0] - PEERS * blocks
    mine = [arrived[field_rows(DECAY, b, blocks), :] for b in range(blocks)]
    theirs = [other[pl.ds(start + b, PEERS, stride=blocks), :] for b in range(blocks)]
    mine, theirs = (
        jnp.concatenate([take_rows(part, place_of) for part in parts], 1)
        for parts in (mine, theirs)
    )
    first = lax.axis_index("pair") == 0
    decay_rows = [jnp.where(first, mine, theirs), jnp.where(first, theirs, mine)]

    def before(values):
        return neighbour_rows(values, SUM_ORDER, -1)

    def after(values):
        return neighbour_rows(values, SUM_ORDER, 1)

    def east(values):
        return pltpu.roll(values, lon - 1, 1)

    def west(values):
        return pltpu.roll(values, 1, 1)

    aligned = [summed(0, 0), summed(0, 1)]
    conductance = [summed(1, 0), summed(1, 1)]
    faces = []
    middle = 0.5 * (conductance[0] + conductance[1])
    north = (0.5 * (conductance[0] + before(conductance[1])), middle)
    south = (middle, 0.5 * (conductance[1] + after(conductance[0])))
    level = []
    for lat in range(2):
        here = conductance[lat]
        east_face = 0.5 * (here + east(here))
        west_face = 0.5 * (here + west(here))
        diagonal = decay_rows[lat] + north[lat] + south[lat] + east_face + west_face
        inverse = 1.0 / diagonal
        faces.append([f * inverse for f in (north[lat], south[lat], east_face, west_face)])
        aligned[lat] = aligned[lat] * inverse
        level.append(aligned[lat])
    for _ in range(SWEEPS - 1):
        around = ((before(level[1]), level[1]), (level[0], after(level[0])))
        level = [
            (aligned[lat] + faces[lat][0] * around[lat][0] + faces[lat][1] * around[lat][1])
            + (faces[lat][2] * east(level[lat]) + faces[lat][3] * west(level[lat]))
            for lat in range(2)
        ]
    me = lax.axis_index(RING)
    for lat in range(2):
        potential[lat : lat + 1] = jnp.sum(
            jnp.where(ring == me, level[lat], 0.0), axis=0, keepdims=True
        )
    for lat in range(2):
        for b, span in enumerate(blocks_of(blocks)):
            at = pl.ds(lat * blocks + b, PEERS, stride=rows)
            tables[0, at, :] = level[lat][:, span]
            tables[1, at, :] = conductance[lat][:, span]
    for half in range(cell_rows // PEERS):
        part = slice(half * PEERS, (half + 1) * PEERS)
        for k in range(2):
            taken = jnp.zeros((PEERS, LANES), jnp.float32)
            for place, device in enumerate(SUM_ORDER):
                for r in range(rows):
                    at = place * rows + r
                    one = pick_lanes(tables[k, at : at + 1, :], lane[part])
                    taken = jnp.where(row[part] == device * rows + r + 1, one, taken)
            for r in range(PEERS):
                theta, b = divmod(half * PEERS + r, blocks)
                boundary[k, 0, theta : theta + 1, blocks_of(blocks)[b]] = taken[r : r + 1]


def shape_of(*dims):
    return jax.ShapeDtypeStruct(dims, jnp.float32)


def exchange(chunks, axes, order):
    return lax.all_to_all(
        chunks, axes, split_axis=0, concat_axis=0, axis_index_groups=[order], tiled=True
    )


def short_plan(
    induction_vector,
    ohmic_spreading_number,
    reciprocal_surface,
    number_per_volume,
    thermal_kelvin,
    mapped_brick_members,
    arrival_owner_map,
    pedersen_sheet,
    electric_decay_rate,
):
    lists = mapped_brick_members[0, 0]
    owners = arrival_owner_map[0, 0]
    lat_rows, lon = electric_decay_rate.shape
    blocks = lon // LANES
    theta_rows = reciprocal_surface.shape[1]
    chunk_rows = CHUNK_FIELDS * blocks
    arguments = (
        induction_vector,
        reciprocal_surface,
        number_per_volume,
        thermal_kelvin,
        lists,
        owners,
        electric_decay_rate,
        ohmic_spreading_number,
    )
    sent, packet = pl.pallas_call(
        collect_kernel,
        out_shape=(
            shape_of(PEERS, chunk_rows, LANES),
            shape_of(4 * theta_rows * blocks, LANES),
        ),
        in_specs=[pl.BlockSpec(memory_space=pltpu.HBM)] * len(arguments),
        out_specs=(
            pl.BlockSpec(memory_space=pltpu.HBM),
            pl.BlockSpec(memory_space=pltpu.VMEM),
        ),
        scratch_shapes=[pltpu.VMEM(a.shape, a.dtype) for a in arguments]
        + [
            pltpu.VMEM((PEERS, chunk_rows, LANES), jnp.float32),
            pltpu.SemaphoreType.DMA((len(arguments),)),
            pltpu.SemaphoreType.DMA((2,)),
        ],
        compiler_params=KERNEL_PARAMS,
        name="collect",
    )(*[pltpu.with_memory_space_constraint(a, pltpu.HBM) for a in arguments])
    arrived = exchange(sent, RING, SLOT_ORDER).reshape(PEERS * chunk_rows, LANES)
    columns, levels = pl.pallas_call(
        prepare_kernel,
        out_shape=(
            jax.ShapeDtypeStruct((PEERS, lon), jnp.int32),
            shape_of(lat_rows * blocks, LANES),
        ),
        in_specs=[pl.BlockSpec(memory_space=pltpu.HBM)] * 2,
        scratch_shapes=[
            pltpu.VMEM(owners.shape, jnp.int32),
            pltpu.VMEM(pedersen_sheet.shape, jnp.float32),
            pltpu.SemaphoreType.DMA((2,)),
        ],
        compiler_params=KERNEL_PARAMS,
        name="prepare",
    )(*[pltpu.with_memory_space_constraint(a, pltpu.HBM) for a in (owners, pedersen_sheet)])
    even = lax.ppermute(packet, RING, [(i, i ^ 1) for i in range(PEERS)])
    odd_pairs = [(i, i + 1) for i in range(1, PEERS - 1, 2)]
    odd = lax.ppermute(packet, RING, odd_pairs + [(j, i) for i, j in odd_pairs])
    arrived, even, columns, levels = lax.optimization_barrier((arrived, even, columns, levels))
    copies = 2 * PEERS
    sum_rows = 2 * lat_rows * blocks
    sums = pl.pallas_call(
        deposit_kernel,
        out_shape=shape_of(copies, sum_rows, LANES),
        compiler_params=KERNEL_PARAMS,
        name="deposit",
    )(arrived, columns, levels)
    decays = arrived.reshape(PEERS, chunk_rows, LANES)[:, DECAY * blocks : (DECAY + 1) * blocks]
    own = jnp.concatenate([packet, even, odd, decays.reshape(PEERS * blocks, LANES)], 0)
    other = lax.ppermute(own, "pair", [(0, 1), (1, 0)])
    gathered = exchange(
        sums, GROUP, [2 * d + p for d in SUM_ORDER for p in SUM_PAIRS]
    ).reshape(copies * sum_rows, LANES)
    found = pl.pallas_call(
        functools.partial(footpoint_kernel, lat_rows=lat_rows),
        out_shape=jax.ShapeDtypeStruct((2 * theta_rows * blocks, LANES), jnp.int32),
        compiler_params=KERNEL_PARAMS,
        name="footpoints",
    )(arrived, lists)
    advanced = pl.pallas_call(
        advance_kernel,
        out_shape=shape_of(3, 1, theta_rows, lon),
        scratch_shapes=[pltpu.VMEM((2, 2, 4, blocks, 8 * theta_rows, LANES), jnp.float32)],
        compiler_params=KERNEL_PARAMS,
        name="advance",
    )(own, other)
    boundary, potential = pl.pallas_call(
        solve_kernel,
        out_shape=(shape_of(2, 1, theta_rows, lon), shape_of(lat_rows, lon)),
        scratch_shapes=[pltpu.VMEM((2, PEERS * lat_rows * blocks, LANES), jnp.float32)],
        compiler_params=KERNEL_PARAMS,
        name="solve",
    )(gathered, arrived, other, found)
    return advanced, boundary, potential


def local(*arguments):
    lists, decay, surface = arguments[5], arguments[8], arguments[2]
    fits = (
        lists.shape[2:] == (PEERS, decay.shape[1])
        and decay.shape == (2, 4 * LANES)
        and surface.shape == (1, 4, 4 * LANES)
        and lax.axis_size("pair") == 2
    )
    return short_plan(*arguments) if fits else stepwise(*arguments)


def solution(mesh):
    in_specs = (
        P(None, ("run", "pair"), ("tile", "sub"), None),
        P(("run", "pair"), ("tile", "sub"), None),
        P(("run", "pair"), ("tile", "sub"), None),
        P(("run", "pair"), ("tile", "sub"), None),
        P(("run", "pair"), ("tile", "sub"), None),
        P(("run", "pair"), ("tile", "sub"), None, None),
        P(("run", "pair"), ("tile", "sub"), None, None),
        P(("run", "pair"), ("tile", "sub"), None),
        P(("run", "tile", "sub"), None),
    )
    out_specs = (
        P(None, ("run", "pair"), ("tile", "sub"), None),
        P(None, ("run", "pair"), ("tile", "sub"), None),
        P(("run", "tile", "sub"), None),
    )
    return jax.shard_map(local, mesh=mesh, in_specs=in_specs, out_specs=out_specs, check_vma=False)
```

```python
import functools

import jax
import jax.numpy as jnp
from jax import lax
from jax.experimental import pallas as pl
from jax.experimental.pallas import tpu as pltpu
from jax.sharding import PartitionSpec as P

DIFF_STEPS = 4
SWEEPS = 8


def extended(cells, sides, width):
    for axis, dim in sides:
        count = lax.axis_size(axis)
        ends = count - 1
        head = lax.slice_in_dim(cells, 0, width, axis=dim)
        tail = lax.slice_in_dim(cells, cells.shape[dim] - width, cells.shape[dim], axis=dim)
        cells = jnp.concatenate(
            [
                lax.ppermute(tail, axis, [(i, (i + 1) % count) for i in range(ends)]),
                cells,
                lax.ppermute(head, axis, [((i + 1) % count, i) for i in range(ends)]),
            ],
            axis=dim,
        )
    return cells


def extend_cells(current_state):
    return extended(current_state, ((("tile", "sub"), 2), ("pair", 1)), 1)


def extend_columns(grid_values):
    return extended(grid_values, ((("tile", "sub"), 0),), 1)


def advance_field(current_state, padded, ohmic_spreading_number):
    neighbours = (
        padded[:, 2:, 1:-1] + padded[:, :-2, 1:-1] + padded[:, 1:-1, 2:] + padded[:, 1:-1, :-2]
    )
    neighbours = neighbours + jnp.roll(current_state, -1, 3) + jnp.roll(current_state, 1, 3)
    return current_state + ohmic_spreading_number * (neighbours - 6.0 * current_state)


def stepwise(
    induction_vector,
    ohmic_spreading_number,
    reciprocal_surface,
    number_per_volume,
    thermal_kelvin,
    mapped_brick_members,
    arrival_owner_map,
    pedersen_sheet,
    electric_decay_rate,
):
    padded = extend_cells(induction_vector)
    theta_diff = padded[2, 1:-1, 2:] - padded[2, 1:-1, :-2]
    phi_diff = jnp.roll(induction_vector[1], -1, 2) - jnp.roll(induction_vector[1], 1, 2)
    current = 0.5 * reciprocal_surface * (theta_diff - phi_diff)
    precipitation_power = 0.25 * number_per_volume * jnp.sqrt(thermal_kelvin)
    cell_lists = mapped_brick_members[0, 0]
    is_listed = cell_lists >= 0
    safe_index = jnp.where(is_listed, cell_lists, 0)
    sources = jnp.stack([current.reshape(-1), precipitation_power.reshape(-1)])
    payload = jnp.where(is_listed[None], sources[:, safe_index], 0.0)
    arrived = lax.all_to_all(payload, ("tile", "sub"), split_axis=1, concat_axis=1, tiled=True)
    land_columns = arrival_owner_map[0, 0]
    lat_rows, lon_cells = electric_decay_rate.shape
    column_count = lat_rows * lon_cells
    column_terms = (
        jnp.zeros((2, column_count), jnp.float32)
        .at[:, land_columns.reshape(-1)]
        .add(arrived.reshape(2, -1))
    )
    local_conductance = jnp.sum(pedersen_sheet, axis=0) + column_terms[1].reshape(
        lat_rows, lon_cells
    )
    aligned_current, conductance = lax.psum(
        (column_terms[0].reshape(lat_rows, lon_cells), local_conductance), "pair"
    )
    advanced = advance_field(induction_vector, padded, ohmic_spreading_number)
    for step_index in range(1, DIFF_STEPS):
        advanced = advance_field(advanced, extend_cells(advanced), ohmic_spreading_number)
    cond_rim = extend_columns(conductance)
    north_face = 0.5 * (conductance + cond_rim[:-2])
    south_face = 0.5 * (conductance + cond_rim[2:])
    east_face = 0.5 * (conductance + jnp.roll(conductance, -1, 1))
    west_face = 0.5 * (conductance + jnp.roll(conductance, 1, 1))
    diagonal = electric_decay_rate + north_face + south_face + east_face + west_face
    potential = aligned_current / diagonal
    for sweep_index in range(SWEEPS - 1):
        potential_rim = extend_columns(potential)
        potential = (
            aligned_current
            + north_face * potential_rim[:-2]
            + south_face * potential_rim[2:]
            + east_face * jnp.roll(potential, -1, 1)
            + west_face * jnp.roll(potential, 1, 1)
        ) / diagonal
    column_values = jnp.stack([potential, conductance]).reshape(2, -1)
    returned = lax.all_to_all(
        column_values[:, land_columns], ("tile", "sub"), split_axis=1, concat_axis=1, tiled=True
    )
    cell_count = current.size
    target = jnp.where(is_listed, cell_lists, cell_count)
    boundary = jnp.zeros((2, cell_count), jnp.float32).at[:, target].add(returned, mode="drop")
    boundary = boundary.reshape((2,) + current.shape)
    return (advanced, boundary, potential)


LANES = 128
PEERS = 8
RING = ("tile", "sub")
GROUP = ("tile", "sub", "pair")
CURRENT, FLUX, RIM_WEIGHT, CELL, OWNER, FIRST_ROW, LAST_ROW, DECAY = range(8)
CHUNK_FIELDS = 8
KERNEL_PARAMS = pltpu.CompilerParams(vmem_limit_bytes=4 * 2**20)


SLOT_ORDER = [5, 4, 3, 2, 1, 0, 7, 6]
SUM_ORDER = [5, 0, 3, 1, 7, 2, 4, 6]
SUM_PAIRS = (1, 0)


def by_position(values, width=LANES):
    row = lax.broadcasted_iota(jnp.int32, (PEERS, width), 0)
    out = jnp.zeros((PEERS, width), jnp.int32)
    for k, value in enumerate(values):
        out = jnp.where(row == k, value, out)
    return out


def take_rows(values, index):
    return jnp.take_along_axis(values, index, axis=0, mode="promise_in_bounds")


def neighbour_rows(values, order, step):
    wanted = [d + step for d in order]
    inside = [0 <= d < PEERS for d in wanted]
    index = by_position([order.index(d) if ok else 0 for d, ok in zip(wanted, inside)])
    valid = by_position([int(ok) for ok in inside]) == 1
    columns = blocks_of(values.shape[1] // LANES)
    return jnp.concatenate(
        [jnp.where(valid, take_rows(values[:, c], index), 0.0) for c in columns], 1
    )


def pick_lanes(row, lane):
    return jnp.take_along_axis(
        jnp.broadcast_to(row, lane.shape), lane, axis=1, mode="promise_in_bounds"
    )


def blocks_of(count):
    return [slice(b * LANES, (b + 1) * LANES) for b in range(count)]


def field_rows(field, block, blocks):
    return pl.ds(field * blocks + block, PEERS, stride=CHUNK_FIELDS * blocks)


def three_terms(values):
    first = values.astype(jnp.bfloat16)
    rest = values - first.astype(jnp.float32)
    second = rest.astype(jnp.bfloat16)
    third = (rest - second.astype(jnp.float32)).astype(jnp.bfloat16)
    return first, second, third


def one_hot_sums(rows, lanes, terms, row_count):
    total = None
    slots = rows.shape[1]
    row_at = lax.broadcasted_iota(jnp.int32, (row_count, slots), 0)
    lane_at = lax.broadcasted_iota(jnp.int32, (LANES, slots), 0)
    for s in range(rows.shape[0]):
        here = row_at == rows[s : s + 1]
        left = jnp.concatenate(
            [
                jnp.where(here, jnp.broadcast_to(t[s : s + 1], here.shape), 0.0)
                for t in terms
            ],
            axis=0,
        ).astype(jnp.bfloat16)
        right = jnp.where(lane_at == lanes[s : s + 1], 1.0, 0.0).astype(jnp.bfloat16)
        part = lax.dot_general(
            left, right, (((1,), (1,)), ((), ())), preferred_element_type=jnp.float32
        )
        total = part if total is None else total + part
    return total


def collect_kernel(*refs):
    count = 8
    here, (sent, packet), mine, (built, arrival, departure) = (
        refs[:count],
        refs[count : count + 2],
        refs[count + 2 : 2 * count + 2],
        refs[2 * count + 2 :],
    )
    copies = [pltpu.make_async_copy(here[k], mine[k], arrival.at[k]) for k in range(count)]
    for copy in copies:
        copy.start()
    for copy in copies:
        copy.wait()
    field, reciprocal, number, kelvin, lists, owners, decay, spreading = mine
    theta_rows, lon = reciprocal.shape[1:]
    blocks = lon // LANES
    spans = blocks_of(blocks)
    toward_theta = field[2, 0]
    toward_phi = field[1, 0]
    order = by_position(SLOT_ORDER)
    own_decay = jnp.where(lax.axis_index("pair") == 0, decay[0:1], decay[1:2])
    for b, span in enumerate(spans):
        built[:, OWNER * blocks + b, :] = take_rows(owners[:, span], order).astype(jnp.float32)
        for k, row in (
            (FIRST_ROW, toward_theta[:1]),
            (LAST_ROW, toward_theta[-1:]),
            (DECAY, own_decay),
        ):
            built[:, k * blocks + b, :] = jnp.broadcast_to(row[:, span], (PEERS, LANES))
    parts = [slice(OWNER * blocks, CHUNK_FIELDS * blocks), slice(0, OWNER * blocks)]
    leaving = [
        pltpu.make_async_copy(built.at[:, part, :], sent.at[:, part, :], departure.at[k])
        for k, part in enumerate(parts)
    ]
    leaving[0].start()
    zero_row = jnp.zeros((1, lon), jnp.float32)
    half = 0.5 * reciprocal[0]
    theta_diff = jnp.concatenate([toward_theta[1:], zero_row], 0) - jnp.concatenate(
        [zero_row, toward_theta[:-1]], 0
    )
    phi_diff = pltpu.roll(toward_phi, lon - 1, 1) - pltpu.roll(toward_phi, 1, 1)
    current = half * (theta_diff - phi_diff)
    flux = 0.25 * number[0] * jnp.sqrt(kelvin[0])
    for b, span in enumerate(spans):
        cell = take_rows(lists[:, span], order)
        lane = cell & (LANES - 1)
        row = cell >> 7
        taken = [jnp.zeros(cell.shape, jnp.float32)] * 3
        for theta in range(theta_rows):
            for c, source in enumerate(spans):
                here = row == theta * blocks + c
                at = slice(theta, theta + 1)
                tables = [current[at, source], flux[at, source]]
                if theta == 0:
                    tables.append(-half[at, source])
                if theta == theta_rows - 1:
                    tables.append(half[at, source])
                for k, table in enumerate(tables):
                    taken[k] = jnp.where(here, pick_lanes(table, lane), taken[k])
        for k, value in enumerate(taken + [cell.astype(jnp.float32)]):
            built[:, k * blocks + b, :] = value
    leaving[1].start()
    for b, span in enumerate(spans):
        for k in range(4):
            at = (b * 4 + k) * theta_rows
            packet[at : at + theta_rows] = (field[k, 0] if k < 3 else spreading[0])[:, span]
    for copy in leaving:
        copy.wait()


def prepare_kernel(owners, sheet, columns, levels, mine, sheets, arrival):
    copies = [
        pltpu.make_async_copy(owners, mine, arrival.at[0]),
        pltpu.make_async_copy(sheet, sheets, arrival.at[1]),
    ]
    for copy in copies:
        copy.start()
    for copy in copies:
        copy.wait()
    order = by_position(SLOT_ORDER)
    spans = blocks_of(columns.shape[1] // LANES)
    level_sum = jnp.sum(sheets[...], axis=0)
    for b, span in enumerate(spans):
        columns[:, span] = take_rows(mine[:, span], order)
        for i in range(level_sum.shape[0]):
            levels[i * len(spans) + b : i * len(spans) + b + 1] = level_sum[i : i + 1, span]


def deposit_kernel(arrived, columns, levels, sums):
    lon = columns.shape[1]
    blocks = lon // LANES
    rows = levels.shape[0]
    above = [
        neighbour_rows(arrived[field_rows(LAST_ROW, b, blocks), :], SLOT_ORDER, -1) for b in range(blocks)
    ]
    below = [
        neighbour_rows(arrived[field_rows(FIRST_ROW, b, blocks), :], SLOT_ORDER, 1) for b in range(blocks)
    ]
    currents, fluxes = [], []
    for b in range(blocks):
        cell = arrived[field_rows(CELL, b, blocks), :].astype(jnp.int32)
        phi_block = (cell >> 7) & (blocks - 1)
        lane = cell & (LANES - 1)
        rim = jnp.zeros((PEERS, LANES), jnp.float32)
        for c in range(blocks):
            found = jnp.where(
                cell < lon, pick_lanes(above[c], lane), pick_lanes(below[c], lane)
            )
            rim = jnp.where(phi_block == c, found, rim)
        weight = arrived[field_rows(RIM_WEIGHT, b, blocks), :]
        currents.append(arrived[field_rows(CURRENT, b, blocks), :] + weight * rim)
        fluxes.append(arrived[field_rows(FLUX, b, blocks), :])
    column = columns[...]
    terms = three_terms(jnp.concatenate(currents, 1)) + three_terms(jnp.concatenate(fluxes, 1))
    total = one_hot_sums(
        column >> 7, column & (LANES - 1), [t.astype(jnp.float32) for t in terms], rows
    )
    parts = [total[k * rows : (k + 1) * rows] for k in range(6)]
    current = parts[0] + parts[1] + parts[2]
    flux = parts[3] + parts[4] + parts[5]
    both = jnp.concatenate([current, flux + levels[...]], 0)
    for k in range(sums.shape[0]):
        sums[k] = both


def footpoint_kernel(arrived, lists, found, *, lat_rows):
    lon = lists.shape[1]
    blocks = lon // LANES
    owner = jnp.concatenate(
        [arrived[field_rows(OWNER, b, blocks), :] for b in range(blocks)], 1
    ).astype(jnp.int32)
    device = by_position(SLOT_ORDER, lon)
    row = (owner >> 7) + device * (lat_rows * blocks) + 1
    lane = owner & (LANES - 1)
    order = by_position(SLOT_ORDER)
    cell = jnp.concatenate([take_rows(lists[:, span], order) for span in blocks_of(blocks)], 1)
    found[...] = one_hot_sums(
        cell >> 7,
        cell & (LANES - 1),
        [row.astype(jnp.float32), lane.astype(jnp.float32)],
        found.shape[0] // 2,
    ).astype(jnp.int32)


def advance_kernel(own, other, advanced, planes):
    theta_rows = advanced.shape[2]
    spans = blocks_of(advanced.shape[3] // LANES)
    span_rows = len(spans) * 4 * theta_rows
    top, here = 2 * theta_rows, slice(2 * theta_rows, 6 * theta_rows)
    is_odd = (lax.axis_index(RING) & 1) == 1
    margin = jnp.zeros((2 * theta_rows, LANES), jnp.float32)
    for shell, bricks in enumerate((own, other)):
        for k in range(4):
            for b in range(len(spans)):
                at = (shell, k, b)
                start = (b * 4 + k) * theta_rows
                middle = bricks[start : start + theta_rows]
                by_even = bricks[span_rows + start : span_rows + start + theta_rows]
                by_odd = bricks[2 * span_rows + start : 2 * span_rows + start + theta_rows]
                for buffer in range(2):
                    planes[buffer, *at, :top] = margin
                    planes[buffer, *at, 6 * theta_rows :] = margin
                planes[0, *at, 4 * theta_rows : 6 * theta_rows] = margin
                planes[0, *at, top : top + theta_rows] = jnp.where(is_odd, by_even, by_odd)
                planes[0, *at, top + theta_rows : top + 2 * theta_rows] = middle
                planes[0, *at, top + 2 * theta_rows : top + 3 * theta_rows] = jnp.where(
                    is_odd, by_odd, by_even
                )
    lane = lax.broadcasted_iota(jnp.int32, (4 * theta_rows, LANES), 1)
    first, last = lane == 0, lane == LANES - 1
    for step in range(DIFF_STEPS):
        now, later = step % 2, 1 - step % 2
        for k in range(3):
            for shell in range(2):
                if step == DIFF_STEPS - 1 and shell == 1:
                    continue
                state = [planes[now, shell, k, b, here] for b in range(len(spans))]
                ahead = [pltpu.roll(x, LANES - 1, 1) for x in state]
                behind = [pltpu.roll(x, 1, 1) for x in state]
                for b, span in enumerate(spans):
                    at = (now, shell, k, b)
                    around = planes[now, 1 - shell, k, b, here] + planes[
                        *at, top + 1 : 6 * theta_rows + 1
                    ]
                    around = around + planes[*at, top - 1 : 6 * theta_rows - 1]
                    around = around + jnp.where(last, ahead[(b + 1) % len(spans)], ahead[b])
                    around = around + jnp.where(first, behind[b - 1], behind[b])
                    spreading = planes[0, shell, 3, b, here]
                    result = state[b] + spreading * (around - 6.0 * state[b])
                    if step == DIFF_STEPS - 1:
                        advanced[k, 0, :, span] = result[theta_rows : 2 * theta_rows]
                    else:
                        planes[later, shell, k, b, here] = result


def solve_kernel(sums, arrived, other, found, boundary, potential, tables):
    lon = potential.shape[1]
    blocks = lon // LANES
    rows = 2 * blocks
    cell_rows = boundary.shape[2] * blocks
    row, lane = found[:cell_rows], found[cell_rows:]
    ring = by_position(SUM_ORDER, lon)
    place_of = by_position([SLOT_ORDER.index(d) for d in SUM_ORDER])

    def summed(term, lat):
        return jnp.concatenate(
            [
                sum(
                    sums[pl.ds((pair * 2 + term) * rows + lat * blocks + b, PEERS, stride=4 * rows), :]
                    for pair in range(2)
                )
                for b in range(blocks)
            ],
            1,
        )

    start = other.shape[0] - PEERS * blocks
    mine = [arrived[field_rows(DECAY, b, blocks), :] for b in range(blocks)]
    theirs = [other[pl.ds(start + b, PEERS, stride=blocks), :] for b in range(blocks)]
    mine, theirs = (
        jnp.concatenate([take_rows(part, place_of) for part in parts], 1)
        for parts in (mine, theirs)
    )
    first = lax.axis_index("pair") == 0
    decay_rows = [jnp.where(first, mine, theirs), jnp.where(first, theirs, mine)]

    def before(values):
        return neighbour_rows(values, SUM_ORDER, -1)

    def after(values):
        return neighbour_rows(values, SUM_ORDER, 1)

    def east(values):
        return pltpu.roll(values, lon - 1, 1)

    def west(values):
        return pltpu.roll(values, 1, 1)

    aligned = [summed(0, 0), summed(0, 1)]
    conductance = [summed(1, 0), summed(1, 1)]
    faces = []
    middle = 0.5 * (conductance[0] + conductance[1])
    north = (0.5 * (conductance[0] + before(conductance[1])), middle)
    south = (middle, 0.5 * (conductance[1] + after(conductance[0])))
    level = []
    for lat in range(2):
        here = conductance[lat]
        east_face = 0.5 * (here + east(here))
        west_face = 0.5 * (here + west(here))
        diagonal = decay_rows[lat] + north[lat] + south[lat] + east_face + west_face
        inverse = 1.0 / diagonal
        faces.append([f * inverse for f in (north[lat], south[lat], east_face, west_face)])
        aligned[lat] = aligned[lat] * inverse
        level.append(aligned[lat])
    for _ in range(SWEEPS - 1):
        around = ((before(level[1]), level[1]), (level[0], after(level[0])))
        level = [
            (aligned[lat] + faces[lat][0] * around[lat][0] + faces[lat][1] * around[lat][1])
            + (faces[lat][2] * east(level[lat]) + faces[lat][3] * west(level[lat]))
            for lat in range(2)
        ]
    me = lax.axis_index(RING)
    for lat in range(2):
        potential[lat : lat + 1] = jnp.sum(
            jnp.where(ring == me, level[lat], 0.0), axis=0, keepdims=True
        )
    for lat in range(2):
        for b, span in enumerate(blocks_of(blocks)):
            at = pl.ds(lat * blocks + b, PEERS, stride=rows)
            tables[0, at, :] = level[lat][:, span]
            tables[1, at, :] = conductance[lat][:, span]
    for half in range(cell_rows // PEERS):
        part = slice(half * PEERS, (half + 1) * PEERS)
        for k in range(2):
            taken = jnp.zeros((PEERS, LANES), jnp.float32)
            for place, device in enumerate(SUM_ORDER):
                for r in range(rows):
                    at = place * rows + r
                    one = pick_lanes(tables[k, at : at + 1, :], lane[part])
                    taken = jnp.where(row[part] == device * rows + r + 1, one, taken)
            for r in range(PEERS):
                theta, b = divmod(half * PEERS + r, blocks)
                boundary[k, 0, theta : theta + 1, blocks_of(blocks)[b]] = taken[r : r + 1]


def shape_of(*dims):
    return jax.ShapeDtypeStruct(dims, jnp.float32)


def exchange(chunks, axes, order):
    return lax.all_to_all(
        chunks, axes, split_axis=0, concat_axis=0, axis_index_groups=[order], tiled=True
    )


def short_plan(
    induction_vector,
    ohmic_spreading_number,
    reciprocal_surface,
    number_per_volume,
    thermal_kelvin,
    mapped_brick_members,
    arrival_owner_map,
    pedersen_sheet,
    electric_decay_rate,
):
    lists = mapped_brick_members[0, 0]
    owners = arrival_owner_map[0, 0]
    lat_rows, lon = electric_decay_rate.shape
    blocks = lon // LANES
    theta_rows = reciprocal_surface.shape[1]
    chunk_rows = CHUNK_FIELDS * blocks
    arguments = (
        induction_vector,
        reciprocal_surface,
        number_per_volume,
        thermal_kelvin,
        lists,
        owners,
        electric_decay_rate,
        ohmic_spreading_number,
    )
    sent, packet = pl.pallas_call(
        collect_kernel,
        out_shape=(
            shape_of(PEERS, chunk_rows, LANES),
            shape_of(4 * theta_rows * blocks, LANES),
        ),
        in_specs=[pl.BlockSpec(memory_space=pltpu.HBM)] * len(arguments),
        out_specs=(
            pl.BlockSpec(memory_space=pltpu.HBM),
            pl.BlockSpec(memory_space=pltpu.VMEM),
        ),
        scratch_shapes=[pltpu.VMEM(a.shape, a.dtype) for a in arguments]
        + [
            pltpu.VMEM((PEERS, chunk_rows, LANES), jnp.float32),
            pltpu.SemaphoreType.DMA((len(arguments),)),
            pltpu.SemaphoreType.DMA((2,)),
        ],
        compiler_params=KERNEL_PARAMS,
        name="collect",
    )(*[pltpu.with_memory_space_constraint(a, pltpu.HBM) for a in arguments])
    arrived = exchange(sent, RING, SLOT_ORDER).reshape(PEERS * chunk_rows, LANES)
    columns, levels = pl.pallas_call(
        prepare_kernel,
        out_shape=(
            jax.ShapeDtypeStruct((PEERS, lon), jnp.int32),
            shape_of(lat_rows * blocks, LANES),
        ),
        in_specs=[pl.BlockSpec(memory_space=pltpu.HBM)] * 2,
        scratch_shapes=[
            pltpu.VMEM(owners.shape, jnp.int32),
            pltpu.VMEM(pedersen_sheet.shape, jnp.float32),
            pltpu.SemaphoreType.DMA((2,)),
        ],
        compiler_params=KERNEL_PARAMS,
        name="prepare",
    )(*[pltpu.with_memory_space_constraint(a, pltpu.HBM) for a in (owners, pedersen_sheet)])
    even = lax.ppermute(packet, RING, [(i, i ^ 1) for i in range(PEERS)])
    odd_pairs = [(i, i + 1) for i in range(1, PEERS - 1, 2)]
    odd = lax.ppermute(packet, RING, odd_pairs + [(j, i) for i, j in odd_pairs])
    arrived, columns, levels = lax.optimization_barrier((arrived, columns, levels))
    copies = 2 * PEERS
    sum_rows = 2 * lat_rows * blocks
    sums = pl.pallas_call(
        deposit_kernel,
        out_shape=shape_of(copies, sum_rows, LANES),
        compiler_params=KERNEL_PARAMS,
        name="deposit",
    )(arrived, columns, levels)
    decays = arrived.reshape(PEERS, chunk_rows, LANES)[:, DECAY * blocks : (DECAY + 1) * blocks]
    own = jnp.concatenate([packet, even, odd, decays.reshape(PEERS * blocks, LANES)], 0)
    other = lax.ppermute(own, "pair", [(0, 1), (1, 0)])
    gathered = exchange(
        sums, GROUP, [2 * d + p for d in SUM_ORDER for p in SUM_PAIRS]
    ).reshape(copies * sum_rows, LANES)
    found = pl.pallas_call(
        functools.partial(footpoint_kernel, lat_rows=lat_rows),
        out_shape=jax.ShapeDtypeStruct((2 * theta_rows * blocks, LANES), jnp.int32),
        compiler_params=KERNEL_PARAMS,
        name="footpoints",
    )(arrived, lists)
    advanced = pl.pallas_call(
        advance_kernel,
        out_shape=shape_of(3, 1, theta_rows, lon),
        scratch_shapes=[pltpu.VMEM((2, 2, 4, blocks, 8 * theta_rows, LANES), jnp.float32)],
        compiler_params=KERNEL_PARAMS,
        name="advance",
    )(own, other)
    boundary, potential = pl.pallas_call(
        solve_kernel,
        out_shape=(shape_of(2, 1, theta_rows, lon), shape_of(lat_rows, lon)),
        scratch_shapes=[pltpu.VMEM((2, PEERS * lat_rows * blocks, LANES), jnp.float32)],
        compiler_params=KERNEL_PARAMS,
        name="solve",
    )(gathered, arrived, other, found)
    return advanced, boundary, potential


def local(*arguments):
    lists, decay, surface = arguments[5], arguments[8], arguments[2]
    fits = (
        lists.shape[2:] == (PEERS, decay.shape[1])
        and decay.shape == (2, 4 * LANES)
        and surface.shape == (1, 4, 4 * LANES)
        and lax.axis_size("pair") == 2
    )
    return short_plan(*arguments) if fits else stepwise(*arguments)


def solution(mesh):
    in_specs = (
        P(None, ("run", "pair"), ("tile", "sub"), None),
        P(("run", "pair"), ("tile", "sub"), None),
        P(("run", "pair"), ("tile", "sub"), None),
        P(("run", "pair"), ("tile", "sub"), None),
        P(("run", "pair"), ("tile", "sub"), None),
        P(("run", "pair"), ("tile", "sub"), None, None),
        P(("run", "pair"), ("tile", "sub"), None, None),
        P(("run", "pair"), ("tile", "sub"), None),
        P(("run", "tile", "sub"), None),
    )
    out_specs = (
        P(None, ("run", "pair"), ("tile", "sub"), None),
        P(None, ("run", "pair"), ("tile", "sub"), None),
        P(("run", "tile", "sub"), None),
    )
    return jax.shard_map(local, mesh=mesh, in_specs=in_specs, out_specs=out_specs, check_vma=False)
```

```python
import functools

import jax
import jax.numpy as jnp
from jax import lax
from jax.experimental import pallas as pl
from jax.experimental.pallas import tpu as pltpu
from jax.sharding import PartitionSpec as P

DIFF_STEPS = 4
SWEEPS = 8


def extended(cells, sides, width):
    for axis, dim in sides:
        count = lax.axis_size(axis)
        ends = count - 1
        head = lax.slice_in_dim(cells, 0, width, axis=dim)
        tail = lax.slice_in_dim(cells, cells.shape[dim] - width, cells.shape[dim], axis=dim)
        cells = jnp.concatenate(
            [
                lax.ppermute(tail, axis, [(i, (i + 1) % count) for i in range(ends)]),
                cells,
                lax.ppermute(head, axis, [((i + 1) % count, i) for i in range(ends)]),
            ],
            axis=dim,
        )
    return cells


def extend_cells(current_state):
    return extended(current_state, ((("tile", "sub"), 2), ("pair", 1)), 1)


def extend_columns(grid_values):
    return extended(grid_values, ((("tile", "sub"), 0),), 1)


def advance_field(current_state, padded, ohmic_spreading_number):
    neighbours = (
        padded[:, 2:, 1:-1] + padded[:, :-2, 1:-1] + padded[:, 1:-1, 2:] + padded[:, 1:-1, :-2]
    )
    neighbours = neighbours + jnp.roll(current_state, -1, 3) + jnp.roll(current_state, 1, 3)
    return current_state + ohmic_spreading_number * (neighbours - 6.0 * current_state)


def stepwise(
    induction_vector,
    ohmic_spreading_number,
    reciprocal_surface,
    number_per_volume,
    thermal_kelvin,
    mapped_brick_members,
    arrival_owner_map,
    pedersen_sheet,
    electric_decay_rate,
):
    padded = extend_cells(induction_vector)
    theta_diff = padded[2, 1:-1, 2:] - padded[2, 1:-1, :-2]
    phi_diff = jnp.roll(induction_vector[1], -1, 2) - jnp.roll(induction_vector[1], 1, 2)
    current = 0.5 * reciprocal_surface * (theta_diff - phi_diff)
    precipitation_power = 0.25 * number_per_volume * jnp.sqrt(thermal_kelvin)
    cell_lists = mapped_brick_members[0, 0]
    is_listed = cell_lists >= 0
    safe_index = jnp.where(is_listed, cell_lists, 0)
    sources = jnp.stack([current.reshape(-1), precipitation_power.reshape(-1)])
    payload = jnp.where(is_listed[None], sources[:, safe_index], 0.0)
    arrived = lax.all_to_all(payload, ("tile", "sub"), split_axis=1, concat_axis=1, tiled=True)
    land_columns = arrival_owner_map[0, 0]
    lat_rows, lon_cells = electric_decay_rate.shape
    column_count = lat_rows * lon_cells
    column_terms = (
        jnp.zeros((2, column_count), jnp.float32)
        .at[:, land_columns.reshape(-1)]
        .add(arrived.reshape(2, -1))
    )
    local_conductance = jnp.sum(pedersen_sheet, axis=0) + column_terms[1].reshape(
        lat_rows, lon_cells
    )
    aligned_current, conductance = lax.psum(
        (column_terms[0].reshape(lat_rows, lon_cells), local_conductance), "pair"
    )
    advanced = advance_field(induction_vector, padded, ohmic_spreading_number)
    for step_index in range(1, DIFF_STEPS):
        advanced = advance_field(advanced, extend_cells(advanced), ohmic_spreading_number)
    cond_rim = extend_columns(conductance)
    north_face = 0.5 * (conductance + cond_rim[:-2])
    south_face = 0.5 * (conductance + cond_rim[2:])
    east_face = 0.5 * (conductance + jnp.roll(conductance, -1, 1))
    west_face = 0.5 * (conductance + jnp.roll(conductance, 1, 1))
    diagonal = electric_decay_rate + north_face + south_face + east_face + west_face
    potential = aligned_current / diagonal
    for sweep_index in range(SWEEPS - 1):
        potential_rim = extend_columns(potential)
        potential = (
            aligned_current
            + north_face * potential_rim[:-2]
            + south_face * potential_rim[2:]
            + east_face * jnp.roll(potential, -1, 1)
            + west_face * jnp.roll(potential, 1, 1)
        ) / diagonal
    column_values = jnp.stack([potential, conductance]).reshape(2, -1)
    returned = lax.all_to_all(
        column_values[:, land_columns], ("tile", "sub"), split_axis=1, concat_axis=1, tiled=True
    )
    cell_count = current.size
    target = jnp.where(is_listed, cell_lists, cell_count)
    boundary = jnp.zeros((2, cell_count), jnp.float32).at[:, target].add(returned, mode="drop")
    boundary = boundary.reshape((2,) + current.shape)
    return (advanced, boundary, potential)


LANES = 128
PEERS = 8
RING = ("tile", "sub")
GROUP = ("tile", "sub", "pair")
CURRENT, FLUX, RIM_WEIGHT, CELL, OWNER, FIRST_ROW, LAST_ROW, DECAY = range(8)
CHUNK_FIELDS = 8
KERNEL_PARAMS = pltpu.CompilerParams(vmem_limit_bytes=4 * 2**20)


SLOT_ORDER = [5, 4, 3, 2, 1, 0, 7, 6]
SUM_ORDER = [5, 0, 3, 1, 7, 2, 4, 6]
SUM_PAIRS = (1, 0)


def by_position(values, width=LANES):
    row = lax.broadcasted_iota(jnp.int32, (PEERS, width), 0)
    out = jnp.zeros((PEERS, width), jnp.int32)
    for k, value in enumerate(values):
        out = jnp.where(row == k, value, out)
    return out


def take_rows(values, index):
    return jnp.take_along_axis(values, index, axis=0, mode="promise_in_bounds")


def neighbour_rows(values, order, step):
    wanted = [d + step for d in order]
    inside = [0 <= d < PEERS for d in wanted]
    index = by_position([order.index(d) if ok else 0 for d, ok in zip(wanted, inside)])
    valid = by_position([int(ok) for ok in inside]) == 1
    columns = blocks_of(values.shape[1] // LANES)
    return jnp.concatenate(
        [jnp.where(valid, take_rows(values[:, c], index), 0.0) for c in columns], 1
    )


def pick_lanes(row, lane):
    return jnp.take_along_axis(
        jnp.broadcast_to(row, lane.shape), lane, axis=1, mode="promise_in_bounds"
    )


def blocks_of(count):
    return [slice(b * LANES, (b + 1) * LANES) for b in range(count)]


def field_rows(field, block, blocks):
    return pl.ds(field * blocks + block, PEERS, stride=CHUNK_FIELDS * blocks)


def three_terms(values):
    first = values.astype(jnp.bfloat16)
    rest = values - first.astype(jnp.float32)
    second = rest.astype(jnp.bfloat16)
    third = (rest - second.astype(jnp.float32)).astype(jnp.bfloat16)
    return first, second, third


def one_hot_sums(rows, lanes, terms, row_count):
    total = None
    slots = rows.shape[1]
    row_at = lax.broadcasted_iota(jnp.int32, (row_count, slots), 0)
    lane_at = lax.broadcasted_iota(jnp.int32, (LANES, slots), 0)
    for s in range(rows.shape[0]):
        here = row_at == rows[s : s + 1]
        left = jnp.concatenate(
            [
                jnp.where(here, jnp.broadcast_to(t[s : s + 1], here.shape), 0.0)
                for t in terms
            ],
            axis=0,
        ).astype(jnp.bfloat16)
        right = jnp.where(lane_at == lanes[s : s + 1], 1.0, 0.0).astype(jnp.bfloat16)
        part = lax.dot_general(
            left, right, (((1,), (1,)), ((), ())), preferred_element_type=jnp.float32
        )
        total = part if total is None else total + part
    return total


def collect_kernel(*refs):
    count = 8
    here, (sent, packet), mine, (built, arrival, departure) = (
        refs[:count],
        refs[count : count + 2],
        refs[count + 2 : 2 * count + 2],
        refs[2 * count + 2 :],
    )
    copies = [pltpu.make_async_copy(here[k], mine[k], arrival.at[k]) for k in range(count)]
    for copy in copies:
        copy.start()
    for copy in copies:
        copy.wait()
    field, reciprocal, number, kelvin, lists, owners, decay, spreading = mine
    theta_rows, lon = reciprocal.shape[1:]
    blocks = lon // LANES
    spans = blocks_of(blocks)
    toward_theta = field[2, 0]
    toward_phi = field[1, 0]
    order = by_position(SLOT_ORDER)
    own_decay = jnp.where(lax.axis_index("pair") == 0, decay[0:1], decay[1:2])
    for b, span in enumerate(spans):
        built[:, OWNER * blocks + b, :] = take_rows(owners[:, span], order).astype(jnp.float32)
        for k, row in (
            (FIRST_ROW, toward_theta[:1]),
            (LAST_ROW, toward_theta[-1:]),
            (DECAY, own_decay),
        ):
            built[:, k * blocks + b, :] = jnp.broadcast_to(row[:, span], (PEERS, LANES))
    parts = [slice(OWNER * blocks, CHUNK_FIELDS * blocks), slice(0, OWNER * blocks)]
    leaving = [
        pltpu.make_async_copy(built.at[:, part, :], sent.at[:, part, :], departure.at[k])
        for k, part in enumerate(parts)
    ]
    leaving[0].start()
    zero_row = jnp.zeros((1, lon), jnp.float32)
    half = 0.5 * reciprocal[0]
    theta_diff = jnp.concatenate([toward_theta[1:], zero_row], 0) - jnp.concatenate(
        [zero_row, toward_theta[:-1]], 0
    )
    phi_diff = pltpu.roll(toward_phi, lon - 1, 1) - pltpu.roll(toward_phi, 1, 1)
    current = half * (theta_diff - phi_diff)
    flux = 0.25 * number[0] * jnp.sqrt(kelvin[0])
    for b, span in enumerate(spans):
        cell = take_rows(lists[:, span], order)
        lane = cell & (LANES - 1)
        row = cell >> 7
        taken = [jnp.zeros(cell.shape, jnp.float32)] * 3
        for theta in range(theta_rows):
            for c, source in enumerate(spans):
                here = row == theta * blocks + c
                at = slice(theta, theta + 1)
                tables = [current[at, source], flux[at, source]]
                if theta == 0:
                    tables.append(-half[at, source])
                if theta == theta_rows - 1:
                    tables.append(half[at, source])
                for k, table in enumerate(tables):
                    taken[k] = jnp.where(here, pick_lanes(table, lane), taken[k])
        for k, value in enumerate(taken + [cell.astype(jnp.float32)]):
            built[:, k * blocks + b, :] = value
    leaving[1].start()
    for b, span in enumerate(spans):
        for k in range(4):
            at = (b * 4 + k) * theta_rows
            packet[at : at + theta_rows] = (field[k, 0] if k < 3 else spreading[0])[:, span]
    for copy in leaving:
        copy.wait()


def prepare_kernel(owners, sheet, columns, levels, mine, sheets, arrival):
    copies = [
        pltpu.make_async_copy(owners, mine, arrival.at[0]),
        pltpu.make_async_copy(sheet, sheets, arrival.at[1]),
    ]
    for copy in copies:
        copy.start()
    for copy in copies:
        copy.wait()
    order = by_position(SLOT_ORDER)
    spans = blocks_of(columns.shape[1] // LANES)
    level_sum = jnp.sum(sheets[...], axis=0)
    for b, span in enumerate(spans):
        columns[:, span] = take_rows(mine[:, span], order)
        for i in range(level_sum.shape[0]):
            levels[i * len(spans) + b : i * len(spans) + b + 1] = level_sum[i : i + 1, span]


def deposit_kernel(arrived, columns, levels, sums):
    lon = columns.shape[1]
    blocks = lon // LANES
    rows = levels.shape[0]
    above = [
        neighbour_rows(arrived[field_rows(LAST_ROW, b, blocks), :], SLOT_ORDER, -1) for b in range(blocks)
    ]
    below = [
        neighbour_rows(arrived[field_rows(FIRST_ROW, b, blocks), :], SLOT_ORDER, 1) for b in range(blocks)
    ]
    currents, fluxes = [], []
    for b in range(blocks):
        cell = arrived[field_rows(CELL, b, blocks), :].astype(jnp.int32)
        phi_block = (cell >> 7) & (blocks - 1)
        lane = cell & (LANES - 1)
        rim = jnp.zeros((PEERS, LANES), jnp.float32)
        for c in range(blocks):
            found = jnp.where(
                cell < lon, pick_lanes(above[c], lane), pick_lanes(below[c], lane)
            )
            rim = jnp.where(phi_block == c, found, rim)
        weight = arrived[field_rows(RIM_WEIGHT, b, blocks), :]
        currents.append(arrived[field_rows(CURRENT, b, blocks), :] + weight * rim)
        fluxes.append(arrived[field_rows(FLUX, b, blocks), :])
    column = columns[...]
    terms = three_terms(jnp.concatenate(currents, 1)) + three_terms(jnp.concatenate(fluxes, 1))
    total = one_hot_sums(
        column >> 7, column & (LANES - 1), [t.astype(jnp.float32) for t in terms], rows
    )
    parts = [total[k * rows : (k + 1) * rows] for k in range(6)]
    current = parts[0] + parts[1] + parts[2]
    flux = parts[3] + parts[4] + parts[5]
    both = jnp.concatenate([current, flux + levels[...]], 0)
    for k in range(sums.shape[0]):
        sums[k] = both


def footpoint_kernel(arrived, lists, found, *, lat_rows):
    lon = lists.shape[1]
    blocks = lon // LANES
    owner = jnp.concatenate(
        [arrived[field_rows(OWNER, b, blocks), :] for b in range(blocks)], 1
    ).astype(jnp.int32)
    device = by_position(SLOT_ORDER, lon)
    row = (owner >> 7) + device * (lat_rows * blocks) + 1
    lane = owner & (LANES - 1)
    order = by_position(SLOT_ORDER)
    cell = jnp.concatenate([take_rows(lists[:, span], order) for span in blocks_of(blocks)], 1)
    found[...] = one_hot_sums(
        cell >> 7,
        cell & (LANES - 1),
        [row.astype(jnp.float32), lane.astype(jnp.float32)],
        found.shape[0] // 2,
    ).astype(jnp.int32)


def advance_kernel(own, other, advanced, planes):
    theta_rows = advanced.shape[2]
    spans = blocks_of(advanced.shape[3] // LANES)
    span_rows = len(spans) * 4 * theta_rows
    top, here = 2 * theta_rows, slice(2 * theta_rows, 6 * theta_rows)
    is_odd = (lax.axis_index(RING) & 1) == 1
    margin = jnp.zeros((2 * theta_rows, LANES), jnp.float32)
    for shell, bricks in enumerate((own, other)):
        for k in range(4):
            for b in range(len(spans)):
                at = (shell, k, b)
                start = (b * 4 + k) * theta_rows
                middle = bricks[start : start + theta_rows]
                by_even = bricks[2 * span_rows + start : 2 * span_rows + start + theta_rows]
                by_odd = bricks[span_rows + start : span_rows + start + theta_rows]
                for buffer in range(2):
                    planes[buffer, *at, :top] = margin
                    planes[buffer, *at, 6 * theta_rows :] = margin
                planes[0, *at, 4 * theta_rows : 6 * theta_rows] = margin
                planes[0, *at, top : top + theta_rows] = jnp.where(is_odd, by_even, by_odd)
                planes[0, *at, top + theta_rows : top + 2 * theta_rows] = middle
                planes[0, *at, top + 2 * theta_rows : top + 3 * theta_rows] = jnp.where(
                    is_odd, by_odd, by_even
                )
    lane = lax.broadcasted_iota(jnp.int32, (4 * theta_rows, LANES), 1)
    first, last = lane == 0, lane == LANES - 1
    for step in range(DIFF_STEPS):
        now, later = step % 2, 1 - step % 2
        for k in range(3):
            for shell in range(2):
                if step == DIFF_STEPS - 1 and shell == 1:
                    continue
                state = [planes[now, shell, k, b, here] for b in range(len(spans))]
                ahead = [pltpu.roll(x, LANES - 1, 1) for x in state]
                behind = [pltpu.roll(x, 1, 1) for x in state]
                for b, span in enumerate(spans):
                    at = (now, shell, k, b)
                    around = planes[now, 1 - shell, k, b, here] + planes[
                        *at, top + 1 : 6 * theta_rows + 1
                    ]
                    around = around + planes[*at, top - 1 : 6 * theta_rows - 1]
                    around = around + jnp.where(last, ahead[(b + 1) % len(spans)], ahead[b])
                    around = around + jnp.where(first, behind[b - 1], behind[b])
                    spreading = planes[0, shell, 3, b, here]
                    result = state[b] + spreading * (around - 6.0 * state[b])
                    if step == DIFF_STEPS - 1:
                        advanced[k, 0, :, span] = result[theta_rows : 2 * theta_rows]
                    else:
                        planes[later, shell, k, b, here] = result


def solve_kernel(sums, arrived, other, found, boundary, potential, tables):
    lon = potential.shape[1]
    blocks = lon // LANES
    rows = 2 * blocks
    cell_rows = boundary.shape[2] * blocks
    row, lane = found[:cell_rows], found[cell_rows:]
    ring = by_position(SUM_ORDER, lon)
    place_of = by_position([SLOT_ORDER.index(d) for d in SUM_ORDER])

    def summed(term, lat):
        return jnp.concatenate(
            [
                sum(
                    sums[pl.ds((pair * 2 + term) * rows + lat * blocks + b, PEERS, stride=4 * rows), :]
                    for pair in range(2)
                )
                for b in range(blocks)
            ],
            1,
        )

    start = other.shape[0] - PEERS * blocks
    mine = [arrived[field_rows(DECAY, b, blocks), :] for b in range(blocks)]
    theirs = [other[pl.ds(start + b, PEERS, stride=blocks), :] for b in range(blocks)]
    mine, theirs = (
        jnp.concatenate([take_rows(part, place_of) for part in parts], 1)
        for parts in (mine, theirs)
    )
    first = lax.axis_index("pair") == 0
    decay_rows = [jnp.where(first, mine, theirs), jnp.where(first, theirs, mine)]

    def before(values):
        return neighbour_rows(values, SUM_ORDER, -1)

    def after(values):
        return neighbour_rows(values, SUM_ORDER, 1)

    def east(values):
        return pltpu.roll(values, lon - 1, 1)

    def west(values):
        return pltpu.roll(values, 1, 1)

    aligned = [summed(0, 0), summed(0, 1)]
    conductance = [summed(1, 0), summed(1, 1)]
    faces = []
    middle = 0.5 * (conductance[0] + conductance[1])
    north = (0.5 * (conductance[0] + before(conductance[1])), middle)
    south = (middle, 0.5 * (conductance[1] + after(conductance[0])))
    level = []
    for lat in range(2):
        here = conductance[lat]
        east_face = 0.5 * (here + east(here))
        west_face = 0.5 * (here + west(here))
        diagonal = decay_rows[lat] + north[lat] + south[lat] + east_face + west_face
        inverse = 1.0 / diagonal
        faces.append([f * inverse for f in (north[lat], south[lat], east_face, west_face)])
        aligned[lat] = aligned[lat] * inverse
        level.append(aligned[lat])
    for _ in range(SWEEPS - 1):
        around = ((before(level[1]), level[1]), (level[0], after(level[0])))
        level = [
            (aligned[lat] + faces[lat][0] * around[lat][0] + faces[lat][1] * around[lat][1])
            + (faces[lat][2] * east(level[lat]) + faces[lat][3] * west(level[lat]))
            for lat in range(2)
        ]
    me = lax.axis_index(RING)
    for lat in range(2):
        potential[lat : lat + 1] = jnp.sum(
            jnp.where(ring == me, level[lat], 0.0), axis=0, keepdims=True
        )
    for lat in range(2):
        for b, span in enumerate(blocks_of(blocks)):
            at = pl.ds(lat * blocks + b, PEERS, stride=rows)
            tables[0, at, :] = level[lat][:, span]
            tables[1, at, :] = conductance[lat][:, span]
    for half in range(cell_rows // PEERS):
        part = slice(half * PEERS, (half + 1) * PEERS)
        for k in range(2):
            taken = jnp.zeros((PEERS, LANES), jnp.float32)
            for place, device in enumerate(SUM_ORDER):
                for r in range(rows):
                    at = place * rows + r
                    one = pick_lanes(tables[k, at : at + 1, :], lane[part])
                    taken = jnp.where(row[part] == device * rows + r + 1, one, taken)
            for r in range(PEERS):
                theta, b = divmod(half * PEERS + r, blocks)
                boundary[k, 0, theta : theta + 1, blocks_of(blocks)[b]] = taken[r : r + 1]


def shape_of(*dims):
    return jax.ShapeDtypeStruct(dims, jnp.float32)


def exchange(chunks, axes, order):
    return lax.all_to_all(
        chunks, axes, split_axis=0, concat_axis=0, axis_index_groups=[order], tiled=True
    )


def short_plan(
    induction_vector,
    ohmic_spreading_number,
    reciprocal_surface,
    number_per_volume,
    thermal_kelvin,
    mapped_brick_members,
    arrival_owner_map,
    pedersen_sheet,
    electric_decay_rate,
):
    lists = mapped_brick_members[0, 0]
    owners = arrival_owner_map[0, 0]
    lat_rows, lon = electric_decay_rate.shape
    blocks = lon // LANES
    theta_rows = reciprocal_surface.shape[1]
    chunk_rows = CHUNK_FIELDS * blocks
    arguments = (
        induction_vector,
        reciprocal_surface,
        number_per_volume,
        thermal_kelvin,
        lists,
        owners,
        electric_decay_rate,
        ohmic_spreading_number,
    )
    sent, packet = pl.pallas_call(
        collect_kernel,
        out_shape=(
            shape_of(PEERS, chunk_rows, LANES),
            shape_of(4 * theta_rows * blocks, LANES),
        ),
        in_specs=[pl.BlockSpec(memory_space=pltpu.HBM)] * len(arguments),
        out_specs=(
            pl.BlockSpec(memory_space=pltpu.HBM),
            pl.BlockSpec(memory_space=pltpu.VMEM),
        ),
        scratch_shapes=[pltpu.VMEM(a.shape, a.dtype) for a in arguments]
        + [
            pltpu.VMEM((PEERS, chunk_rows, LANES), jnp.float32),
            pltpu.SemaphoreType.DMA((len(arguments),)),
            pltpu.SemaphoreType.DMA((2,)),
        ],
        compiler_params=KERNEL_PARAMS,
        name="collect",
    )(*[pltpu.with_memory_space_constraint(a, pltpu.HBM) for a in arguments])
    arrived = exchange(sent, RING, SLOT_ORDER).reshape(PEERS * chunk_rows, LANES)
    columns, levels = pl.pallas_call(
        prepare_kernel,
        out_shape=(
            jax.ShapeDtypeStruct((PEERS, lon), jnp.int32),
            shape_of(lat_rows * blocks, LANES),
        ),
        in_specs=[pl.BlockSpec(memory_space=pltpu.HBM)] * 2,
        scratch_shapes=[
            pltpu.VMEM(owners.shape, jnp.int32),
            pltpu.VMEM(pedersen_sheet.shape, jnp.float32),
            pltpu.SemaphoreType.DMA((2,)),
        ],
        compiler_params=KERNEL_PARAMS,
        name="prepare",
    )(*[pltpu.with_memory_space_constraint(a, pltpu.HBM) for a in (owners, pedersen_sheet)])
    even = lax.ppermute(packet, RING, [(i, i ^ 1) for i in range(PEERS)])
    odd_pairs = [(i, i + 1) for i in range(1, PEERS - 1, 2)]
    odd = lax.ppermute(packet, RING, odd_pairs + [(j, i) for i, j in odd_pairs])
    arrived, columns, levels = lax.optimization_barrier((arrived, columns, levels))
    copies = 2 * PEERS
    sum_rows = 2 * lat_rows * blocks
    sums = pl.pallas_call(
        deposit_kernel,
        out_shape=shape_of(copies, sum_rows, LANES),
        compiler_params=KERNEL_PARAMS,
        name="deposit",
    )(arrived, columns, levels)
    decays = arrived.reshape(PEERS, chunk_rows, LANES)[:, DECAY * blocks : (DECAY + 1) * blocks]
    own = jnp.concatenate([packet, odd, even, decays.reshape(PEERS * blocks, LANES)], 0)
    other = lax.ppermute(own, "pair", [(0, 1), (1, 0)])
    gathered = exchange(
        sums, GROUP, [2 * d + p for d in SUM_ORDER for p in SUM_PAIRS]
    ).reshape(copies * sum_rows, LANES)
    found = pl.pallas_call(
        functools.partial(footpoint_kernel, lat_rows=lat_rows),
        out_shape=jax.ShapeDtypeStruct((2 * theta_rows * blocks, LANES), jnp.int32),
        compiler_params=KERNEL_PARAMS,
        name="footpoints",
    )(arrived, lists)
    advanced = pl.pallas_call(
        advance_kernel,
        out_shape=shape_of(3, 1, theta_rows, lon),
        scratch_shapes=[pltpu.VMEM((2, 2, 4, blocks, 8 * theta_rows, LANES), jnp.float32)],
        compiler_params=KERNEL_PARAMS,
        name="advance",
    )(own, other)
    boundary, potential = pl.pallas_call(
        solve_kernel,
        out_shape=(shape_of(2, 1, theta_rows, lon), shape_of(lat_rows, lon)),
        scratch_shapes=[pltpu.VMEM((2, PEERS * lat_rows * blocks, LANES), jnp.float32)],
        compiler_params=KERNEL_PARAMS,
        name="solve",
    )(gathered, arrived, other, found)
    return advanced, boundary, potential


def local(*arguments):
    lists, decay, surface = arguments[5], arguments[8], arguments[2]
    fits = (
        lists.shape[2:] == (PEERS, decay.shape[1])
        and decay.shape == (2, 4 * LANES)
        and surface.shape == (1, 4, 4 * LANES)
        and lax.axis_size("pair") == 2
    )
    return short_plan(*arguments) if fits else stepwise(*arguments)


def solution(mesh):
    in_specs = (
        P(None, ("run", "pair"), ("tile", "sub"), None),
        P(("run", "pair"), ("tile", "sub"), None),
        P(("run", "pair"), ("tile", "sub"), None),
        P(("run", "pair"), ("tile", "sub"), None),
        P(("run", "pair"), ("tile", "sub"), None),
        P(("run", "pair"), ("tile", "sub"), None, None),
        P(("run", "pair"), ("tile", "sub"), None, None),
        P(("run", "pair"), ("tile", "sub"), None),
        P(("run", "tile", "sub"), None),
    )
    out_specs = (
        P(None, ("run", "pair"), ("tile", "sub"), None),
        P(None, ("run", "pair"), ("tile", "sub"), None),
        P(("run", "tile", "sub"), None),
    )
    return jax.shard_map(local, mesh=mesh, in_specs=in_specs, out_specs=out_specs, check_vma=False)
```
